512 devices in a mesh: freq: 4 (over x), row: 8 (over z), col: 16 (over y, core).
Axes of the slice: x: 4, y: 8, z: 8, core: 2. Of those that a mesh axis runs over, the one named last changes fastest.
Arguments:
- traces: bfloat16 [2048, 2048, 128], P(('freq', 'row', 'col')), may hold values from -6 to 6
- source_inverse: float32 [2, 16], replicated, may hold values from 0.5 to 1.5
Outputs:
- multiples: bfloat16 [2048, 2048, 128], P(('freq', 'row', 'col'))
The draws below stay inside these ranges and needn't reach their ends.
All inputs are finite; a program needn't handle non-finite values.
Results may differ from the reference program's by a relative error of at most 0.0084.
Values may be sent and summed in bfloat16 or wider, within the bound.
A program may use at most 64 MiB of HBM per device.

```python
import math
import jax
import jax.numpy as jnp
from jax import lax

NS = 2048
NT = 128
NF = 16


def block_levels(stream_key, extent, shards, smallest, high):
    gain = 1.0
    for dim, parts in shards:
        draws = jax.random.uniform(jax.random.fold_in(jax.random.fold_in(stream_key, 6), dim), (parts,), jnp.float32, smallest / len(shards), high / len(shards))
        gain = gain * jnp.repeat(jnp.exp(draws), extent[dim] // parts).reshape((-1,) + (1,) * (len(extent) - 1 - dim))
    return gain


def bell_draw(key, shape, scale, most, split=(), held_as=jnp.bfloat16):
    array = jax.random.normal(key, shape, jnp.float32) * scale
    if len(split) > 0:
        array = block_levels(key, shape, split, -0.22, 0.18) * array
    return jnp.clip(array, min=-most, max=most).astype(held_as)


def setup_inputs(seed: int = 0) -> dict:
    key_list = jax.random.split(jax.random.key(seed), 3)
    return {
        "traces": bell_draw(key_list[0], (NS, NS, NT), 1.0, 6.0, ((0, 512),)),
        "source_inverse": jnp.clip(jax.random.uniform(key_list[1], (2, NF), jnp.float32, 0.5, 1.5), 0.5, 1.5),
    }


def dft_tables(count, length):
    bins = jnp.arange(count, dtype=jnp.int32) + 1
    times = jnp.arange(length, dtype=jnp.int32)
    index = bins[:, None] * times[None, :] % length
    angle = index.astype(jnp.float32) * (2.0 * math.pi / length)
    cosine = jnp.cos(angle)
    sine = jnp.sin(angle)
    norm = 1.0 / math.sqrt(length)
    stacked = jnp.concatenate([cosine, -sine], 0)
    forward = (stacked * norm).astype(jnp.bfloat16)
    inverse = (stacked * (2.0 * norm)).astype(jnp.bfloat16)
    return (forward, inverse)

def reference(traces, source_inverse):
    count = source_inverse.shape[1]
    forward, inverse = dft_tables(count, NT)
    flat = traces.reshape(NS * NS, NT)
    spectra = jnp.dot(flat, forward.T, preferred_element_type=jnp.float32).astype(jnp.bfloat16)
    spectra = spectra.T.reshape(2, count, NS, NS)
    scale = 1.0 / math.sqrt(NS)
    high = lax.Precision.HIGHEST

    def square(freq_index):
        real = spectra[0, freq_index].astype(jnp.float32)
        imag = spectra[1, freq_index].astype(jnp.float32)
        prod_real = jnp.dot(real, real, precision=high) - jnp.dot(imag, imag, precision=high)
        prod_imag = jnp.dot(real, imag, precision=high) + jnp.dot(imag, real, precision=high)
        w_real = source_inverse[0, freq_index]
        w_imag = source_inverse[1, freq_index]
        pred_real = (w_real * prod_real - w_imag * prod_imag) * scale
        pred_imag = (w_real * prod_imag + w_imag * prod_real) * scale
        return jnp.stack([pred_real, pred_imag]).astype(jnp.bfloat16)
    predicted = lax.map(square, jnp.arange(count, dtype=jnp.int32))
    stacked = jnp.transpose(predicted, (1, 0, 2, 3)).reshape(2 * count, NS * NS)
    result = jnp.dot(stacked.T, inverse, preferred_element_type=jnp.float32)
    return result.astype(jnp.bfloat16).reshape(NS, NS, NT)
```

```python
import functools
import math

import jax
import jax.numpy as jnp
import numpy as np
from jax import lax
from jax.experimental import pallas as pl
from jax.experimental.pallas import tpu as pltpu
from jax.sharding import PartitionSpec as P

MESH = pl.DeviceIdType.MESH
BF16 = jnp.bfloat16
F32 = jnp.float32
VMEM_LIMIT = 44 * 1024 * 1024


def tables(count, length):
    bins = np.arange(count, dtype=np.int32) + 1
    times = np.arange(length, dtype=np.int32)
    index = bins[:, None] * times[None, :] % length
    angle = index.astype(np.float32) * np.float32(2.0 * math.pi / length)
    norm = np.float32(1.0 / math.sqrt(length))
    stacked = np.stack([np.cos(angle), -np.sin(angle)])
    forward = np.zeros((count, 2, 4, 4, length), np.float32)
    backward = np.zeros((count, 2, 2, 4, 2, 4, length), np.float32)
    for i in range(4):
        forward[:, :, i, i] = np.transpose(stacked * norm, (1, 0, 2))
        for h in range(2):
            backward[:, h, :, i, h, i] = np.transpose(stacked * (2 * norm), (1, 0, 2))
    forward = forward.reshape(count * 8, 4 * length)
    backward = backward.reshape(count * 16, 8 * length)
    return forward.astype(jnp.bfloat16), backward.astype(jnp.bfloat16)


def low_rows(shape):
    return lax.broadcasted_iota(jnp.int32, shape, len(shape) - 2) < 4


def interleave(first, second):
    axis = first.ndim - 2
    low = low_rows(first.shape)
    top = jnp.where(low, first, pltpu.roll(second, 4, axis))
    bottom = jnp.where(low, pltpu.roll(first, 4, axis), second)
    return top, bottom


def exchange_kernel(
    scale,
    traces,
    table,
    weights,
    out,
    tr,
    tbl,
    S,
    T,
    R,
    A,
    B,
    W,
    O,
    T2,
    tr_sem,
    tbl_sem,
    in1,
    in2,
    ret1,
    ret2,
    send,
    xr_sem,
    n_sem,
    dp_sem,
    d_sem,
    core_sem,
    own_sem,
):
    x = lax.axis_index("freq")
    z = lax.axis_index("row")
    col = lax.axis_index("col")
    y = col // 2
    c = col % 2
    uy, uz = y % 2, z % 2
    Y, Z = y // 2, z // 2
    u = uy * 2 + uz

    def dev(xx, zz, yy, cc):
        return (xx, zz, yy * 2 + cc)

    def along(axis_pos, other_pos, core):
        return (
            jnp.where(core == 0, axis_pos, other_pos),
            jnp.where(core == 0, other_pos, axis_pos),
        )

    def remote(src, dst, s, r, to):
        return pltpu.make_async_remote_copy(
            src_ref=src, dst_ref=dst, send_sem=s, recv_sem=r, device_id=to, device_id_type=MESH
        )

    def wait_bytes(ref, sem):
        pltpu.make_async_copy(ref, ref, sem).wait()

    tbl_copy = pltpu.make_async_copy(table, tbl, tbl_sem)
    tbl_copy.start()
    for k in range(8):
        pltpu.make_async_copy(traces.at[:, pl.ds(k * 256, 256), :], tr.at[k], tr_sem.at[k]).start()

    barrier = pltpu.get_barrier_semaphore()
    partner = dev(x, z, y, 1 - c)
    left = dev((x + 3) % 4, z, y, c)
    right = dev((x + 1) % 4, z, y, c)
    yn = dev(x, z, y + 1 - 2 * uy, c)
    zn = dev(x, z + 1 - 2 * uz, y, c)
    dn = dev(x, z + 1 - 2 * uz, y + 1 - 2 * uy, c)

    def greet(d, carry):
        for core in range(2):
            pl.semaphore_signal(barrier, inc=1, device_id=dev(x, z, (y + d) % 8, core), device_id_type=MESH)
            pl.semaphore_signal(barrier, inc=1, device_id=dev(x, (z + d) % 8, y, core), device_id_type=MESH)
        return carry

    lax.fori_loop(1, 8, greet, 0)
    for other in (partner, left, right, dn):
        pl.semaphore_signal(barrier, inc=1, device_id=other, device_id_type=MESH)

    tbl_copy.wait()

    def transform(core, v):
        k = core * 4 + v
        pltpu.make_async_copy(tr.at[k], tr.at[k], tr_sem.at[k]).wait()
        block = jnp.concatenate([tr[k, s] for s in range(4)], axis=1)
        data = lax.dot_general(tbl[...], block, (((1,), (1,)), ((), ())), preferred_element_type=F32)
        data = data.reshape(16, 8, 256)
        data = jnp.concatenate([data[:, :, :128], data[:, :, 128:]], axis=1)
        data = data.astype(BF16).reshape(4, 4, 16, 128)
        for first in range(4):
            if core == 0:
                S[first, :, v] = data[first]
            else:
                S[4:8, first, v] = data[first]

    for v in range(4):
        transform(0, v)
    pl.semaphore_wait(barrier, 32)

    for d in range(1, 4):
        to = (Y + d) % 4
        remote(S.at[to], T.at[:, Y, c], send.at[0], in1, dev(x, z, 2 * to + uy, 0)).start()

    @pl.when(c == 0)
    def _():
        pltpu.make_async_copy(S.at[Y], T.at[:, Y, c], in1).start()

    @pl.when(c == 1)
    def _():
        remote(S.at[Y], T.at[:, Y, c], send.at[0], in1, partner).start()

    for v in range(4):
        transform(1, v)
    for d in range(1, 4):
        to = (Z + d) % 4
        remote(S.at[4 + to], T.at[:, Z, c], send.at[0], in1, dev(x, 2 * to + uz, y, 1)).start()

    @pl.when(c == 1)
    def _():
        pltpu.make_async_copy(S.at[4 + Z], T.at[:, Z, c], in1).start()

    @pl.when(c == 0)
    def _():
        remote(S.at[4 + Z], T.at[:, Z, c], send.at[0], in1, partner).start()

    wait_bytes(T, in1)

    b4 = jnp.where(c == 0, Z, Y)
    for d in range(1, 4):
        to = (b4 + d) % 4
        far = 2 * to + jnp.where(c == 0, uz, uy)
        yy = jnp.where(c == 0, y, far)
        zz = jnp.where(c == 0, far, z)
        remote(T.at[to], R.at[b4], send.at[1], in2, dev(x, zz, yy, c)).start()
    pltpu.make_async_copy(T.at[b4], R.at[b4], in2).start()
    wait_bytes(R, in2)

    def settle(n, carry):
        b, a = n // 4, n % 4
        row = pl.multiple_of(jnp.where(c == 0, a * 4 + b, n) * 16, 16)
        first = R[b, a, 0].astype(F32).reshape(4, 2, 8, 128)
        second = R[b, a, 1].astype(F32).reshape(4, 2, 8, 128)
        real, imag = interleave(first, second)
        for v in range(4):
            for h in range(2):
                tile = jnp.concatenate([real[v, h], imag[v, h]], axis=0).astype(BF16)
                A[c, u, pl.ds(row, 16), v * 256 + h * 128 : v * 256 + h * 128 + 128] = tile
        return carry

    lax.fori_loop(0, 16, settle, 0)

    def lanes(v):
        return pl.ds(pl.multiple_of(v * 256, 256), 256)

    def panel(m, v):
        return A.at[c, m, :, lanes(v)]

    def x_send(m):
        remote(panel(m, u), B.at[x, m], send.at[2], xr_sem.at[0, m], right).start()
        remote(panel(m, u), B.at[x, m], send.at[2], xr_sem.at[1, m], left).start()

    def n_send(which, v):
        remote(panel(u, v), panel(u, v), send.at[3], n_sem.at[which, v], (yn, zn)[which]).start()

    def core_send(ref):
        remote(ref, ref, send.at[4], core_sem, partner).start()

    my, mz, md = u ^ 2, u ^ 1, u ^ 3
    x_send(u)
    n_send(0, my)
    n_send(1, mz)
    remote(panel(u, md), panel(u, md), send.at[3], dp_sem, dn).start()
    core_send(A.at[c, u])
    n_send(0, u)
    n_send(1, u)
    n_send(0, mz)
    n_send(1, my)
    n_send(0, md)
    n_send(1, md)

    def n_arrive(which, v, forward):
        m = (my, mz)[which]
        wait_bytes(panel(m, v), n_sem.at[which, v])
        if forward:
            half = A.at[c, m, pl.ds(which * 128, 128), lanes(v)]
            remote(half, half, send.at[3], d_sem.at[which, v], (zn, yn)[which]).start()
        core_send(panel(m, v))

    n_arrive(0, u, True)
    x_send(my)
    n_arrive(1, u, True)
    x_send(mz)
    wait_bytes(panel(md, u), dp_sem)
    x_send(md)
    core_send(panel(md, u))
    pltpu.make_async_copy(A.at[c, :, :, lanes(u)], B.at[x], own_sem).start()

    xl, xr, xo = (x + 3) % 4, (x + 1) % 4, (x + 2) % 4

    def x_arrive(m, odd):
        wait_bytes(B.at[xl, m], xr_sem.at[0, m])
        if not odd:
            remote(B.at[xl, m], B.at[xl, m], send.at[2], xr_sem.at[2, m], right).start()
        wait_bytes(B.at[xr, m], xr_sem.at[1, m])
        if odd:
            remote(B.at[xr, m], B.at[xr, m], send.at[2], xr_sem.at[2, m], left).start()

    x_arrive(u, False)
    n_arrive(0, my, True)
    n_arrive(1, mz, True)
    x_arrive(my, True)
    n_arrive(0, md, True)
    n_arrive(1, md, True)
    x_arrive(mz, False)
    n_arrive(0, mz, False)
    n_arrive(1, my, False)
    x_arrive(md, True)

    def regroup(xp):
        def step(n, carry):
            uz_, Z_, Y_ = n // 16, (n // 4) % 4, n % 4
            row = pl.multiple_of((Y_ * 4 + Z_) * 16, 16)
            even = B[xp, uz_, pl.ds(row, 16), :].astype(F32)
            odd = B[xp, 2 + uz_, pl.ds(row, 16), :].astype(F32)
            at = pl.ds(pl.multiple_of((2 * Z_ + uz_) * 64 + Y_ * 16, 16), 16)
            W[xp, at, 0:256] = jnp.concatenate([even[:8], odd[:8]], axis=0).astype(BF16)
            W[xp, at, 256:512] = jnp.concatenate([even[8:], odd[8:]], axis=0).astype(BF16)
            return carry

        lax.fori_loop(0, 32, step, 0, unroll=4)

    wait_bytes(B.at[x], own_sem)
    regroup(x)
    regroup(xl)
    regroup(xr)
    for m in (u, my, mz, md):
        wait_bytes(B.at[xo, m], xr_sem.at[2, m])
    regroup(xo)
    for v in (u ^ 1, u ^ 2, u ^ 3):
        for which in range(2):
            half = A.at[c, md, pl.ds(which * 128, 128), lanes(v)]
            wait_bytes(half, d_sem.at[which, v])
            core_send(half)
    wait_bytes(A.at[1 - c], core_sem)

    j = Y * 4 + Z
    w_real, w_imag = weights[0, j], weights[1, j]

    def multiply(m, carry):
        my_, mz_ = m // 2, m % 2
        total = jnp.dot(A[0, m], W[0:2].reshape(1024, 512), preferred_element_type=F32)
        total += jnp.dot(A[1, m], W[2:4].reshape(1024, 512), preferred_element_type=F32)
        total = total.reshape(16, 2, 8, 512)
        real = total[:, 0, :, :256] - total[:, 1, :, 256:]
        imag = total[:, 0, :, 256:] + total[:, 1, :, :256]
        pred_real = (w_real * real - w_imag * imag) * scale
        pred_imag = (w_real * imag + w_imag * real) * scale
        for core, part in enumerate(interleave(pred_real, pred_imag)):
            part = jnp.concatenate([part[:, :, :128], part[:, :, 128:]], axis=1).astype(BF16)
            for n in range(16):
                yy, zz = 2 * (n // 4) + my_, 2 * (n % 4) + mz_
                if core == 0:
                    O[yy, zz] = part[n]
                else:
                    O[8 + zz, yy] = part[n]
        return carry

    lax.fori_loop(0, 4, multiply, 0)

    def back1(d, carry):
        yy, zz = (y + d) % 8, (z + d) % 8
        remote(O.at[yy], T2.at[:, y, c], send.at[5], ret1, dev(x, z, yy, 0)).start()
        remote(O.at[8 + zz], T2.at[:, z, c], send.at[5], ret1, dev(x, zz, y, 1)).start()
        return carry

    lax.fori_loop(1, 8, back1, 0)

    @pl.when(c == 0)
    def _():
        pltpu.make_async_copy(O.at[y], T2.at[:, y, c], ret1).start()
        remote(O.at[8 + z], T2.at[:, z, c], send.at[5], ret1, partner).start()

    @pl.when(c == 1)
    def _():
        pltpu.make_async_copy(O.at[8 + z], T2.at[:, z, c], ret1).start()
        remote(O.at[y], T2.at[:, y, c], send.at[5], ret1, partner).start()

    wait_bytes(T2, ret1)

    b8 = jnp.where(c == 0, z, y)

    def back2(d, carry):
        to = (b8 + d) % 8
        yy = jnp.where(c == 0, y, to)
        zz = jnp.where(c == 0, to, z)
        remote(T2.at[to], out.at[b8], send.at[6], ret2, dev(x, zz, yy, c)).start()
        return carry

    lax.fori_loop(1, 8, back2, 0)
    pltpu.make_async_copy(T2.at[b8], out.at[b8], ret2).start()
    wait_bytes(out, ret2)

    wait_bytes(S.at[pl.ds(0, 7)], send.at[0])
    wait_bytes(T.at[pl.ds(0, 3)], send.at[1])
    wait_bytes(B.at[pl.ds(0, 3)], send.at[2])
    wait_bytes(A.at[0, pl.ds(0, 3)], send.at[3])
    wait_bytes(A.at[0], send.at[4])
    wait_bytes(O.at[pl.ds(0, 15)], send.at[5])
    wait_bytes(T2.at[pl.ds(0, 7)], send.at[6])


def restore_kernel(spectra, table, out):
    n = pl.program_id(0)
    core, uy, uz = n // 4, (n // 2) % 2, n % 2
    c = lax.axis_index("col") % 2
    tiles = []
    for j in range(16):
        y, z = 2 * (j // 4) + uy, 2 * (j % 4) + uz
        b, a = jnp.where(c == 0, z, y), jnp.where(c == 0, y, z)
        tiles.append(spectra[b, a, core])
    left = jnp.concatenate(tiles, axis=0)
    traces = lax.dot_general(left, table[...], (((0,), (0,)), ((), ())), preferred_element_type=F32)
    traces = traces.astype(BF16)
    for h in range(2):
        for s in range(4):
            k = (h * 4 + s) * 128
            out[s, h * 128 : h * 128 + 128, :] = traces[:, k : k + 128]


def on_device(forward, backward, traces, source_inverse):
    hbm = pl.BlockSpec(memory_space=pl.ANY)
    dma = pltpu.SemaphoreType.DMA
    width = traces.shape[1]
    spectra = pl.pallas_call(
        functools.partial(exchange_kernel, 1.0 / math.sqrt(width)),
        out_shape=jax.ShapeDtypeStruct((8, 8, 2, 16, 128), BF16),
        in_specs=[hbm, hbm, pl.BlockSpec(memory_space=pltpu.SMEM)],
        out_specs=hbm,
        scratch_shapes=[
            pltpu.VMEM((8, 4, 256, 128), BF16),
            pltpu.VMEM((128, 512), BF16),
            pltpu.VMEM((8, 4, 4, 16, 128), BF16),
            pltpu.VMEM((4, 4, 2, 4, 16, 128), BF16),
            pltpu.VMEM((4, 4, 2, 4, 16, 128), BF16),
            pltpu.VMEM((2, 4, 256, 1024), BF16),
            pltpu.VMEM((4, 4, 256, 256), BF16),
            pltpu.VMEM((4, 512, 512), BF16),
            pltpu.VMEM((16, 8, 16, 128), BF16),
            pltpu.VMEM((8, 8, 2, 16, 128), BF16),
            dma((8,)),
            dma(()),
            dma(()),
            dma(()),
            dma(()),
            dma(()),
            dma((7,)),
            dma((3, 4)),
            dma((2, 4)),
            dma(()),
            dma((2, 4)),
            dma(()),
            dma(()),
        ],
        compiler_params=pltpu.CompilerParams(
            collective_id=0, has_side_effects=True, vmem_limit_bytes=VMEM_LIMIT
        ),
        name="exchange",
    )(traces, jnp.asarray(forward), source_inverse)
    return pl.pallas_call(
        restore_kernel,
        grid=(8,),
        out_shape=jax.ShapeDtypeStruct(traces.shape, BF16),
        in_specs=[
            pl.BlockSpec((8, 8, 2, 16, 128), lambda n: (0, 0, 0, 0, 0)),
            pl.BlockSpec((256, 1024), lambda n: (0, 0)),
        ],
        out_specs=pl.BlockSpec((4, 256, 128), lambda n: (0, n, 0)),
        compiler_params=pltpu.CompilerParams(vmem_limit_bytes=VMEM_LIMIT),
        name="restore",
    )(spectra, jnp.asarray(backward))


def solution(mesh):
    forward, backward = tables(16, 128)
    in_specs = (P(("freq", "row", "col"), None, None), P())
    out_specs = P(("freq", "row", "col"), None, None)
    return jax.shard_map(
        functools.partial(on_device, forward, backward),
        mesh=mesh,
        in_specs=in_specs,
        out_specs=out_specs,
        check_vma=False,
    )
```

```python
import functools
import math

import jax
import jax.numpy as jnp
import numpy as np
from jax import lax
from jax.experimental import pallas as pl
from jax.experimental.pallas import tpu as pltpu
from jax.sharding import PartitionSpec as P

MESH = pl.DeviceIdType.MESH
BF16 = jnp.bfloat16
F32 = jnp.float32
VMEM_LIMIT = 62 * 1024 * 1024 + 512 * 1024


def tables(count, length):
    bins = np.arange(count, dtype=np.int32) + 1
    times = np.arange(length, dtype=np.int32)
    index = bins[:, None] * times[None, :] % length
    angle = index.astype(np.float32) * np.float32(2.0 * math.pi / length)
    norm = np.float32(1.0 / math.sqrt(length))
    stacked = np.stack([np.cos(angle), -np.sin(angle)])
    forward = np.zeros((count, 2, 4, 4, length), np.float32)
    backward = np.zeros((count, 2, 2, 4, 2, 4, length), np.float32)
    for i in range(4):
        forward[:, :, i, i] = np.transpose(stacked * norm, (1, 0, 2))
        for h in range(2):
            backward[:, h, :, i, h, i] = np.transpose(stacked * (2 * norm), (1, 0, 2))
    forward = forward.reshape(count * 8, 4 * length)
    backward = backward.reshape(count * 16, 8 * length)
    return forward.astype(jnp.bfloat16), backward.astype(jnp.bfloat16)


def low_rows(shape):
    return lax.broadcasted_iota(jnp.int32, shape, len(shape) - 2) < 4


def interleave(first, second):
    axis = first.ndim - 2
    low = low_rows(first.shape)
    top = jnp.where(low, first, pltpu.roll(second, 4, axis))
    bottom = jnp.where(low, pltpu.roll(first, 4, axis), second)
    return top, bottom


def exchange_kernel(
    scale,
    traces,
    table,
    source,
    out,
    tr,
    tbl,
    weights,
    S,
    T,
    R,
    A,
    B,
    W,
    O,
    T2,
    tr_sem,
    tbl_sem,
    src_sem,
    in1,
    in2,
    ret1,
    ret2,
    send,
    x_sem,
    n_sem,
    dp_sem,
    d_sem,
    core_sem,
    own_sem,
):
    x = lax.axis_index("freq")
    z = lax.axis_index("row")
    col = lax.axis_index("col")
    y = col // 2
    c = col % 2
    uy, uz = y % 2, z % 2
    Y, Z = y // 2, z // 2
    u = uy * 2 + uz

    def dev(xx, zz, yy, cc):
        return (xx, zz, yy * 2 + cc)

    def remote(src, dst, s, r, to):
        return pltpu.make_async_remote_copy(
            src_ref=src, dst_ref=dst, send_sem=s, recv_sem=r, device_id=to, device_id_type=MESH
        )

    def local(src, dst, s):
        return pltpu.make_async_copy(src, dst, s)

    def wait_bytes(ref, sem):
        pltpu.make_async_copy(ref, ref, sem).wait()

    local(table, tbl, tbl_sem).start()
    for h in range(2):
        for k in range(4):
            local(traces.at[:, pl.ds(2 * k, 2), h], tr.at[h, k], tr_sem.at[h, k]).start()
    local(source, weights, src_sem).start()

    barrier = pltpu.get_barrier_semaphore()
    partner = dev(x, z, y, 1 - c)
    left = dev((x + 3) % 4, z, y, c)
    right = dev((x + 1) % 4, z, y, c)
    yn = dev(x, z, y + 1 - 2 * uy, c)
    zn = dev(x, z + 1 - 2 * uz, y, c)
    dn = dev(x, z + 1 - 2 * uz, y + 1 - 2 * uy, c)

    def greet(d, carry):
        for core in range(2):
            pl.semaphore_signal(barrier, inc=1, device_id=dev(x, z, (y + d) % 8, core), device_id_type=MESH)
            pl.semaphore_signal(barrier, inc=1, device_id=dev(x, (z + d) % 8, y, core), device_id_type=MESH)
        return carry

    lax.fori_loop(1, 8, greet, 0)
    for other in (partner, left, right, dn):
        pl.semaphore_signal(barrier, inc=1, device_id=other, device_id_type=MESH)

    def transform(h, core):
        for w in range(2):
            k = core * 2 + w
            wait_bytes(tr.at[h, k], tr_sem.at[h, k])
            block = jnp.concatenate([tr[h, k, s].reshape(256, 128) for s in range(4)], axis=1)
            data = lax.dot_general(tbl[...], block, (((1,), (1,)), ((), ())), preferred_element_type=F32)
            data = data.reshape(16, 8, 256)
            data = jnp.concatenate([data[:, :, :128], data[:, :, 128:]], axis=1)
            data = data.astype(BF16).reshape(4, 4, 16, 128)
            for first in range(4):
                if core == 0:
                    S[h, first, :, w] = data[first]
                else:
                    S[h, 4:8, first, w] = data[first]

    def scatter(h):
        for d in range(1, 4):
            to = (Y + d) % 4
            remote(S.at[h, to], T.at[h, :, Y, c], send.at[h], in1.at[h], dev(x, z, 2 * to + uy, 0)).start()
            to = (Z + d) % 4
            remote(S.at[h, 4 + to], T.at[h, :, Z, c], send.at[h], in1.at[h], dev(x, 2 * to + uz, y, 1)).start()

        @pl.when(c == 0)
        def _():
            local(S.at[h, Y], T.at[h, :, Y, c], in1.at[h]).start()
            remote(S.at[h, 4 + Z], T.at[h, :, Z, c], send.at[h], in1.at[h], partner).start()

        @pl.when(c == 1)
        def _():
            local(S.at[h, 4 + Z], T.at[h, :, Z, c], in1.at[h]).start()
            remote(S.at[h, Y], T.at[h, :, Y, c], send.at[h], in1.at[h], partner).start()

    def scatter2(h):
        wait_bytes(T.at[h], in1.at[h])
        b4 = jnp.where(c == 0, Z, Y)
        for d in (1, 3, 2):
            to = (b4 + d) % 4
            far = 2 * to + jnp.where(c == 0, uz, uy)
            yy = jnp.where(c == 0, y, far)
            zz = jnp.where(c == 0, far, z)
            remote(T.at[h, to], R.at[h, b4], send.at[2 + h], in2.at[h], dev(x, zz, yy, c)).start()
        local(T.at[h, b4], R.at[h, b4], in2.at[h]).start()

    def settle(h):
        wait_bytes(R.at[h], in2.at[h])

        def step(n, carry):
            b, a = n // 4, n % 4
            row = pl.multiple_of(jnp.where(c == 0, a * 4 + b, n) * 16, 16)
            first = R[h, b, a, 0].astype(F32).reshape(2, 2, 8, 128)
            second = R[h, b, a, 1].astype(F32).reshape(2, 2, 8, 128)
            real, imag = interleave(first, second)
            for v in range(4):
                tile = jnp.concatenate([real[v // 2, v % 2], imag[v // 2, v % 2]], axis=0).astype(BF16)
                A[c, u, pl.ds(row, 16), v * 256 + h * 128 : v * 256 + h * 128 + 128] = tile
            return carry

        lax.fori_loop(0, 16, step, 0, unroll=2)

    my, mz, md = u ^ 2, u ^ 1, u ^ 3
    xl, xr, xo = (x + 3) % 4, (x + 1) % 4, (x + 2) % 4

    def lanes(v, h):
        return pl.ds(pl.multiple_of(v * 256 + h * 128, 128), 128)

    def panel(m, v, h):
        return A.at[c, m, :, lanes(v, h)]

    def x_send(m, h):
        remote(panel(m, u, h), B.at[x, h, m], send.at[4], x_sem.at[0, h, m], right).start()
        remote(panel(m, u, h), B.at[x, h, m], send.at[4], x_sem.at[1, h, m], left).start()

    def n_send(which, v, h):
        ref = panel(u, v, h)
        remote(ref, ref, send.at[5], n_sem.at[which, v, h], (yn, zn)[which]).start()

    def core_send(m, ref):
        remote(ref, ref, send.at[6], core_sem.at[m], partner).start()

    def first_sends(h):
        x_send(u, h)
        n_send(0, my, h)
        n_send(1, mz, h)
        remote(panel(u, md, h), panel(u, md, h), send.at[5], dp_sem.at[h], dn).start()

    def rest_sends(h):
        n_send(0, u, h)
        n_send(1, u, h)
        n_send(0, mz, h)
        n_send(1, my, h)
        n_send(0, md, h)
        n_send(1, md, h)

    def n_arrive(which, v, h, forward):
        m = (my, mz)[which]
        wait_bytes(panel(m, v, h), n_sem.at[which, v, h])
        if forward:
            half = A.at[c, m, pl.ds(which * 128, 128), lanes(v, h)]
            remote(half, half, send.at[5], d_sem.at[which, v, h], (zn, yn)[which]).start()
        core_send(m, panel(m, v, h))

    def first_arrive(h):
        n_arrive(0, u, h, True)
        x_send(my, h)
        n_arrive(1, u, h, True)
        x_send(mz, h)
        wait_bytes(panel(md, u, h), dp_sem.at[h])
        x_send(md, h)
        core_send(md, panel(md, u, h))
        local(A.at[c, :, :, lanes(u, h)], B.at[x, h], own_sem.at[h]).start()

    def x_arrive(m, h, odd):
        wait_bytes(B.at[xl, h, m], x_sem.at[0, h, m])
        if not odd:
            remote(B.at[xl, h, m], B.at[xl, h, m], send.at[4], x_sem.at[2, h, m], right).start()
        wait_bytes(B.at[xr, h, m], x_sem.at[1, h, m])
        if odd:
            remote(B.at[xr, h, m], B.at[xr, h, m], send.at[4], x_sem.at[2, h, m], left).start()

    def d_arrive(h):
        for r in (1, 2, 3):
            v = u ^ r
            for which in range(2):
                half = A.at[c, md, pl.ds(which * 128, 128), lanes(v, h)]
                wait_bytes(half, d_sem.at[which, v, h])
                core_send(md, half)

    def regroup(xp, h):
        def step(n, carry):
            uz_, Z_, Y_ = n // 16, (n // 4) % 4, n % 4
            row = pl.multiple_of((Y_ * 4 + Z_) * 16, 16)
            even = B[xp, h, uz_, pl.ds(row, 16), :].astype(F32)
            odd = B[xp, h, 2 + uz_, pl.ds(row, 16), :].astype(F32)
            at = pl.ds(pl.multiple_of((2 * Z_ + uz_) * 64 + Y_ * 16, 16), 16)
            W[xp, at, h * 128 : h * 128 + 128] = jnp.concatenate([even[:8], odd[:8]], axis=0).astype(BF16)
            W[xp, at, 256 + h * 128 : 384 + h * 128] = jnp.concatenate([even[8:], odd[8:]], axis=0).astype(BF16)
            return carry

        lax.fori_loop(0, 32, step, 0, unroll=8)

    j = Y * 4 + Z

    def multiply(at, flip):
        m = u ^ flip
        wait_bytes(A.at[1 - c, m], core_sem.at[m])
        w_real, w_imag = weights[0, j], weights[1, j]
        total = jnp.dot(A[0, m], W[0:2].reshape(1024, 512), preferred_element_type=F32)
        total += jnp.dot(A[1, m], W[2:4].reshape(1024, 512), preferred_element_type=F32)
        total = total.reshape(16, 2, 8, 512)
        real = total[:, 0, :, :256] - total[:, 1, :, 256:]
        imag = total[:, 0, :, 256:] + total[:, 1, :, :256]
        pred_real = (w_real * real - w_imag * imag) * scale
        pred_imag = (w_real * imag + w_imag * real) * scale
        for core, part in enumerate(interleave(pred_real, pred_imag)):
            part = jnp.concatenate([part[:, :, :128], part[:, :, 128:]], axis=1).astype(BF16)
            part = part.reshape(4, 4, 16, 128)
            for first in range(4):
                if core == 0:
                    O[at * 8 + first] = part[first]
                else:
                    O[at * 8 + 4 : at * 8 + 8, first] = part[first]

        uy_, uz_ = uy ^ (flip // 2), uz ^ (flip % 2)
        to_y = T2.at[pl.ds(uz_ * 4, 4), y, c]
        to_z = T2.at[pl.ds(uy_ * 4, 4), z, c]
        y_done, z_done = ret1.at[uz_, uy], ret1.at[uy_, uz]
        for d in (1, 3, 2, 0):
            to = (Y + d) % 4
            ref = O.at[at * 8 + to]
            if d == 0 and flip // 2 == 0:

                @pl.when(c == 0)
                def _():
                    local(ref, to_y, y_done).start()

                @pl.when(c == 1)
                def _():
                    remote(ref, to_y, send.at[7], y_done, partner).start()
            else:
                remote(ref, to_y, send.at[7], y_done, dev(x, z, 2 * to + uy_, 0)).start()
            to = (Z + d) % 4
            ref2 = O.at[at * 8 + 4 + to]
            if d == 0 and flip % 2 == 0:

                @pl.when(c == 1)
                def _():
                    local(ref2, to_z, z_done).start()

                @pl.when(c == 0)
                def _():
                    remote(ref2, to_z, send.at[7], z_done, partner).start()
            else:
                remote(ref2, to_z, send.at[7], z_done, dev(x, 2 * to + uz_, y, 1)).start()

    def back2(flip):
        b8 = jnp.where(c == 0, z, y)
        half, parity = b8 // 2, (b8 % 2) ^ flip
        for side in range(2):
            wait_bytes(O.at[pl.ds(0, 8)], ret1.at[parity, side])
        for d in (1, 3, 2, 0):
            to = (half + d) % 4
            ref = T2.at[parity * 4 + to]
            if d == 0 and flip == 0:
                local(ref, out.at[b8], ret2).start()
            else:
                far = 2 * to + parity
                yy = jnp.where(c == 0, y, far)
                zz = jnp.where(c == 0, far, z)
                remote(ref, out.at[b8], send.at[8], ret2, dev(x, zz, yy, c)).start()

    wait_bytes(tbl, tbl_sem)
    transform(0, 0)
    transform(0, 1)
    pl.semaphore_wait(barrier, 32)
    scatter(0)
    transform(1, 0)
    transform(1, 1)
    scatter(1)
    wait_bytes(weights, src_sem)
    scatter2(0)
    scatter2(1)
    settle(0)
    first_sends(0)
    rest_sends(0)
    first_arrive(0)
    settle(1)
    first_sends(1)
    core_send(u, A.at[c, u])
    rest_sends(1)
    x_arrive(u, 0, False)
    n_arrive(0, my, 0, True)
    n_arrive(1, mz, 0, True)
    x_arrive(my, 0, True)
    first_arrive(1)
    wait_bytes(B.at[x, 0], own_sem.at[0])
    regroup(x, 0)
    n_arrive(0, md, 0, True)
    n_arrive(1, md, 0, True)
    x_arrive(mz, 0, False)
    n_arrive(0, mz, 0, False)
    n_arrive(1, my, 0, False)
    x_arrive(md, 0, True)
    regroup(xl, 0)
    regroup(xr, 0)
    x_arrive(u, 1, False)
    n_arrive(0, my, 1, True)
    n_arrive(1, mz, 1, True)
    x_arrive(my, 1, True)
    wait_bytes(B.at[x, 1], own_sem.at[1])
    regroup(x, 1)
    n_arrive(0, md, 1, True)
    n_arrive(1, md, 1, True)
    x_arrive(mz, 1, False)
    n_arrive(0, mz, 1, False)
    n_arrive(1, my, 1, False)
    x_arrive(md, 1, True)
    regroup(xl, 1)
    regroup(xr, 1)
    d_arrive(0)
    for m in (u, my, mz, md):
        wait_bytes(B.at[xo, 0, m], x_sem.at[2, 0, m])
    regroup(xo, 0)
    for m in (u, my, mz, md):
        wait_bytes(B.at[xo, 1, m], x_sem.at[2, 1, m])
    regroup(xo, 1)
    multiply(0, 0)
    multiply(1, 2)
    d_arrive(1)
    multiply(2, 1)
    multiply(3, 3)
    back2(0)
    back2(1)
    wait_bytes(out, ret2)

    for h in range(2):
        wait_bytes(S.at[h, pl.ds(0, 7)], send.at[h])
        wait_bytes(T.at[h, pl.ds(0, 3)], send.at[2 + h])
    wait_bytes(B.at[pl.ds(0, 3)], send.at[4])
    wait_bytes(A.at[0, pl.ds(0, 3)], send.at[5])
    wait_bytes(A.at[0], send.at[6])
    wait_bytes(O.at[pl.ds(0, 30)], send.at[7])
    wait_bytes(T2.at[pl.ds(0, 7)], send.at[8])


def restore_kernel(spectra, table, out, held, sem):
    c = lax.axis_index("col") % 2
    copies = []
    for n in range(8):
        core, uy, uz = n // 4, (n // 2) % 2, n % 2
        tiles = []
        for j in range(16):
            y, z = 2 * (j // 4) + uy, 2 * (j % 4) + uz
            b, a = jnp.where(c == 0, z, y), jnp.where(c == 0, y, z)
            tiles.append(spectra[b, a, core])
        left = jnp.concatenate(tiles, axis=0)
        traces = lax.dot_general(left, table[...], (((0,), (0,)), ((), ())), preferred_element_type=F32)
        traces = traces.astype(BF16)
        for h in range(2):
            for s in range(4):
                k = (h * 4 + s) * 128
                held[s, n * 256 + h * 128 : n * 256 + h * 128 + 128, :] = traces[:, k : k + 128]
        rows = pl.ds(n * 256, 256)
        copy = pltpu.make_async_copy(held.at[:, rows, :], out.at[:, rows, :], sem.at[n])
        copy.start()
        copies.append(copy)
    for copy in copies:
        copy.wait()


def on_device(forward, backward, traces, source_inverse):
    hbm = pl.BlockSpec(memory_space=pltpu.HBM)
    vmem = pl.BlockSpec(memory_space=pltpu.VMEM)
    dma = pltpu.SemaphoreType.DMA
    width = traces.shape[1]
    spectra = pl.pallas_call(
        functools.partial(exchange_kernel, 1.0 / math.sqrt(width)),
        out_shape=jax.ShapeDtypeStruct((8, 8, 2, 16, 128), BF16),
        in_specs=[hbm, hbm, hbm],
        out_specs=vmem,
        scratch_shapes=[
            pltpu.VMEM((2, 4, 4, 2, 128, 128), BF16),
            pltpu.VMEM((128, 512), BF16),
            pltpu.SMEM((2, 16), F32),
            pltpu.VMEM((2, 8, 4, 2, 16, 128), BF16),
            pltpu.VMEM((2, 4, 4, 2, 2, 16, 128), BF16),
            pltpu.VMEM((2, 4, 4, 2, 2, 16, 128), BF16),
            pltpu.VMEM((2, 4, 256, 1024), BF16),
            pltpu.VMEM((4, 2, 4, 256, 128), BF16),
            pltpu.VMEM((4, 512, 512), BF16),
            pltpu.VMEM((32, 4, 16, 128), BF16),
            pltpu.VMEM((8, 8, 2, 16, 128), BF16),
            dma((2, 4)),
            dma(()),
            dma(()),
            dma((2,)),
            dma((2,)),
            dma((2, 2)),
            dma(()),
            dma((9,)),
            dma((3, 2, 4)),
            dma((2, 4, 2)),
            dma((2,)),
            dma((2, 4, 2)),
            dma((4,)),
            dma((2,)),
        ],
        compiler_params=pltpu.CompilerParams(
            collective_id=0, has_side_effects=True, vmem_limit_bytes=VMEM_LIMIT
        ),
        name="exchange",
    )(traces.reshape(4, 8, 2, 128, 128), jnp.asarray(forward), source_inverse)
    return pl.pallas_call(
        restore_kernel,
        out_shape=jax.ShapeDtypeStruct(traces.shape, BF16),
        in_specs=[vmem, vmem],
        out_specs=hbm,
        scratch_shapes=[pltpu.VMEM((4, width, 128), BF16), dma((8,))],
        compiler_params=pltpu.CompilerParams(vmem_limit_bytes=VMEM_LIMIT),
        name="restore",
    )(spectra, jnp.asarray(backward))


def solution(mesh):
    forward, backward = tables(16, 128)
    in_specs = (P(("freq", "row", "col"), None, None), P())
    out_specs = P(("freq", "row", "col"), None, None)
    return jax.shard_map(
        functools.partial(on_device, forward, backward),
        mesh=mesh,
        in_specs=in_specs,
        out_specs=out_specs,
        check_vma=False,
    )
```

```python
import functools
import math

import jax
import jax.numpy as jnp
import numpy as np
from jax import lax
from jax.experimental import pallas as pl
from jax.experimental.pallas import tpu as pltpu
from jax.sharding import PartitionSpec as P

MESH = pl.DeviceIdType.MESH
BF16 = jnp.bfloat16
F32 = jnp.float32
VMEM_LIMIT = 62 * 1024 * 1024 + 512 * 1024


def tables(count, length):
    bins = np.arange(count, dtype=np.int32) + 1
    times = np.arange(length, dtype=np.int32)
    index = bins[:, None] * times[None, :] % length
    angle = index.astype(np.float32) * np.float32(2.0 * math.pi / length)
    norm = np.float32(1.0 / math.sqrt(length))
    stacked = np.stack([np.cos(angle), -np.sin(angle)])
    forward = np.zeros((count, 2, 4, 4, length), np.float32)
    for i in range(4):
        forward[:, :, i, i] = np.transpose(stacked * norm, (1, 0, 2))
    forward = forward.reshape(count * 8, 4 * length)
    return forward.astype(jnp.bfloat16), (2 * forward).astype(jnp.bfloat16)


def low_rows(shape):
    return lax.broadcasted_iota(jnp.int32, shape, len(shape) - 2) < 4


def interleave(first, second):
    axis = first.ndim - 2
    low = low_rows(first.shape)
    top = jnp.where(low, first, pltpu.roll(second, 4, axis))
    bottom = jnp.where(low, pltpu.roll(first, 4, axis), second)
    return top, bottom


def exchange_kernel(
    scale,
    traces,
    table,
    source,
    out,
    tr,
    tbl,
    weights,
    S,
    T,
    R,
    A,
    B,
    W,
    O,
    T2,
    tr_sem,
    tbl_sem,
    src_sem,
    in1,
    in2,
    ret1,
    ret2,
    send,
    x_sem,
    p_sem,
    n_sem,
    dp_sem,
    d_sem,
    core_sem,
    own_sem,
):
    x = lax.axis_index("freq")
    z = lax.axis_index("row")
    col = lax.axis_index("col")
    y = col // 2
    c = col % 2
    uy, uz = y % 2, z % 2
    Y, Z = y // 2, z // 2
    u = uy * 2 + uz

    def dev(xx, zz, yy, cc):
        return (xx, zz, yy * 2 + cc)

    def remote(src, dst, s, r, to):
        return pltpu.make_async_remote_copy(
            src_ref=src, dst_ref=dst, send_sem=s, recv_sem=r, device_id=to, device_id_type=MESH
        )

    def local(src, dst, s):
        return pltpu.make_async_copy(src, dst, s)

    def wait_bytes(ref, sem):
        pltpu.make_async_copy(ref, ref, sem).wait()

    local(table, tbl, tbl_sem).start()
    for h in range(2):
        for k in range(4):
            local(traces.at[:, pl.ds(2 * k, 2), h], tr.at[h, k], tr_sem.at[h, k]).start()
    local(source, weights, src_sem).start()

    barrier = pltpu.get_barrier_semaphore()
    partner = dev(x, z, y, 1 - c)
    left = dev((x + 3) % 4, z, y, c)
    right = dev((x + 1) % 4, z, y, c)
    yn = dev(x, z, y + 1 - 2 * uy, c)
    zn = dev(x, z + 1 - 2 * uz, y, c)
    dn = dev(x, z + 1 - 2 * uz, y + 1 - 2 * uy, c)
    others = [partner, left, right, yn, zn, dn]
    for d in (2, 4, 6):
        a_y, a_z = jnp.where(c == 0, (y + d) % 8, y), jnp.where(c == 0, z, (z + d) % 8)
        b_y, b_z = jnp.where(c == 0, y, (y + d) % 8), jnp.where(c == 0, (z + d) % 8, z)
        others += [dev(x, a_z, a_y, 0), dev(x, a_z, a_y, 1), dev(x, b_z, b_y, c)]
    for other in others:
        pl.semaphore_signal(barrier, inc=1, device_id=other, device_id_type=MESH)

    def transform(h, core):
        for w in range(2):
            k = core * 2 + w
            wait_bytes(tr.at[h, k], tr_sem.at[h, k])
            block = jnp.concatenate([tr[h, k, s].reshape(256, 128) for s in range(4)], axis=1)
            data = lax.dot_general(tbl[...], block, (((1,), (1,)), ((), ())), preferred_element_type=F32)
            data = data.reshape(16, 8, 256)
            data = jnp.concatenate([data[:, :, :128], data[:, :, 128:]], axis=1)
            data = data.astype(BF16).reshape(4, 4, 16, 128)
            for first in range(4):
                if core == 0:
                    S[h, first, :, w] = data[first]
                else:
                    S[h, 4:8, first, w] = data[first]

    def scatter_y(h):
        for d in (2, 1, 3):
            to = (Y + d) % 4
            remote(S.at[h, to], T.at[h, :, Y, c], send.at[h], in1.at[h], dev(x, z, 2 * to + uy, 0)).start()

        @pl.when(c == 0)
        def _():
            local(S.at[h, Y], T.at[h, :, Y, c], in1.at[h]).start()

        @pl.when(c == 1)
        def _():
            remote(S.at[h, Y], T.at[h, :, Y, c], send.at[h], in1.at[h], partner).start()

    def scatter_z(h):
        for d in (2, 1, 3):
            to = (Z + d) % 4
            remote(S.at[h, 4 + to], T.at[h, :, Z, c], send.at[h], in1.at[h], dev(x, 2 * to + uz, y, 1)).start()

        @pl.when(c == 0)
        def _():
            remote(S.at[h, 4 + Z], T.at[h, :, Z, c], send.at[h], in1.at[h], partner).start()

        @pl.when(c == 1)
        def _():
            local(S.at[h, 4 + Z], T.at[h, :, Z, c], in1.at[h]).start()

    def scatter2(h):
        wait_bytes(T.at[h], in1.at[h])
        b4 = jnp.where(c == 0, Z, Y)
        for d in (2, 1, 3):
            to = (b4 + d) % 4
            far = 2 * to + jnp.where(c == 0, uz, uy)
            yy = jnp.where(c == 0, y, far)
            zz = jnp.where(c == 0, far, z)
            remote(T.at[h, to], R.at[h, b4], send.at[2 + h], in2.at[h], dev(x, zz, yy, c)).start()
        local(T.at[h, b4], R.at[h, b4], in2.at[h]).start()

    def settle(h):
        wait_bytes(R.at[h], in2.at[h])

        def step(n, carry):
            b, a = n // 4, n % 4
            row = pl.multiple_of(jnp.where(c == 0, a * 4 + b, n) * 16, 16)
            first = R[h, b, a, 0].astype(F32).reshape(2, 2, 8, 128)
            second = R[h, b, a, 1].astype(F32).reshape(2, 2, 8, 128)
            real, imag = interleave(first, second)
            for v in range(4):
                tile = jnp.concatenate([real[v // 2, v % 2], imag[v // 2, v % 2]], axis=0).astype(BF16)
                A[c, u, pl.ds(row, 16), v * 256 + h * 128 : v * 256 + h * 128 + 128] = tile
            return carry

        lax.fori_loop(0, 16, step, 0, unroll=2)

    my, mz, md = u ^ 2, u ^ 1, u ^ 3
    xl, xr, xo = (x + 3) % 4, (x + 1) % 4, (x + 2) % 4

    def lanes(v, h):
        return pl.ds(pl.multiple_of(v * 256 + h * 128, 128), 128)

    def panel(m, v, rows=pl.ds(0, 256)):
        return A.at[c, m, rows, pl.ds(pl.multiple_of(v * 256, 256), 256)]

    def x_send(m, h):
        ref = A.at[c, m, :, lanes(u, h)]
        remote(ref, B.at[x, h, m], send.at[4], x_sem.at[0, h, m], right).start()
        remote(ref, B.at[x, h, m], send.at[4], x_sem.at[1, h, m], left).start()

    def core_send(m, ref):
        remote(ref, ref, send.at[6], core_sem.at[m], partner).start()

    def first_sends(h):
        x_send(u, h)
        for ref, sem, to in (
            (A.at[c, u, :, lanes(my, h)], p_sem.at[0, h], yn),
            (A.at[c, u, :, lanes(mz, h)], p_sem.at[1, h], zn),
            (A.at[c, u, :, lanes(md, h)], dp_sem.at[h], dn),
        ):
            remote(ref, ref, send.at[5], sem, to).start()

    def first_arrive(h):
        for m, sem in ((my, p_sem.at[0, h]), (mz, p_sem.at[1, h]), (md, dp_sem.at[h])):
            wait_bytes(A.at[c, m, :, lanes(u, h)], sem)
            x_send(m, h)
        local(A.at[c, :, :, lanes(u, h)], B.at[x, h], own_sem.at[h]).start()

    def rest_sends():
        for v0, v1 in ((u, u), (mz, my), (md, md)):
            remote(panel(u, v0), panel(u, v0), send.at[5], n_sem.at[0, v0], yn).start()
            remote(panel(u, v1), panel(u, v1), send.at[5], n_sem.at[1, v1], zn).start()

    def pass_on(which, v):
        m = (my, mz)[which]
        half = panel(m, v, pl.ds(which * 128, 128))
        remote(half, half, send.at[5], d_sem.at[which, v], (zn, yn)[which]).start()

    def n_arrive(which, v, forward):
        m = (my, mz)[which]
        wait_bytes(panel(m, v), n_sem.at[which, v])
        if forward:
            pass_on(which, v)
        core_send(m, panel(m, v))

    def x_arrive(m, h, odd):
        wait_bytes(B.at[xl, h, m], x_sem.at[0, h, m])
        if not odd:
            remote(B.at[xl, h, m], B.at[xl, h, m], send.at[4], x_sem.at[2, h, m], right).start()
        wait_bytes(B.at[xr, h, m], x_sem.at[1, h, m])
        if odd:
            remote(B.at[xr, h, m], B.at[xr, h, m], send.at[4], x_sem.at[2, h, m], left).start()

    def x_far(h):
        for m in (u, my, mz, md):
            wait_bytes(B.at[xo, h, m], x_sem.at[2, h, m])

    def d_arrive():
        for v0, v1 in ((mz, my), (md, md), (my, mz)):
            for which, v in ((0, v0), (1, v1)):
                half = panel(md, v, pl.ds(which * 128, 128))
                wait_bytes(half, d_sem.at[which, v])
                core_send(md, half)

    def regroup(xp, h):
        def step(n, carry):
            uz_, Z_, Y_ = n // 16, (n // 4) % 4, n % 4
            row = pl.multiple_of((Y_ * 4 + Z_) * 16, 16)
            even = B[xp, h, uz_, pl.ds(row, 16), :].astype(F32)
            odd = B[xp, h, 2 + uz_, pl.ds(row, 16), :].astype(F32)
            at = pl.ds(pl.multiple_of((2 * Z_ + uz_) * 64 + Y_ * 16, 16), 16)
            W[xp, at, h * 128 : h * 128 + 128] = jnp.concatenate([even[:8], odd[:8]], axis=0).astype(BF16)
            W[xp, at, 256 + h * 128 : 384 + h * 128] = jnp.concatenate([even[8:], odd[8:]], axis=0).astype(BF16)
            return carry

        lax.fori_loop(0, 32, step, 0, unroll=8)

    j = Y * 4 + Z

    def multiply(at, flip):
        m = u ^ flip
        wait_bytes(A.at[1 - c, m], core_sem.at[m])
        w_real, w_imag = weights[0, j], weights[1, j]
        total = jnp.dot(A[0, m], W[0:2].reshape(1024, 512), preferred_element_type=F32)
        total += jnp.dot(A[1, m], W[2:4].reshape(1024, 512), preferred_element_type=F32)
        total = total.reshape(16, 2, 8, 512)
        real = total[:, 0, :, :256] - total[:, 1, :, 256:]
        imag = total[:, 0, :, 256:] + total[:, 1, :, :256]
        pred_real = (w_real * real - w_imag * imag) * scale
        pred_imag = (w_real * imag + w_imag * real) * scale
        for core, part in enumerate(interleave(pred_real, pred_imag)):
            part = jnp.concatenate([part[:, :, :128], part[:, :, 128:]], axis=1).astype(BF16)
            part = part.reshape(4, 4, 16, 128)
            for first in range(4):
                if core == 0:
                    O[at * 8 + first] = part[first]
                else:
                    O[at * 8 + 4 : at * 8 + 8, first] = part[first]

        uy_, uz_ = uy ^ (flip // 2), uz ^ (flip % 2)
        to_y = T2.at[pl.ds(uz_ * 4, 4), y, c]
        to_z = T2.at[pl.ds(uy_ * 4, 4), z, c]
        y_done, z_done = ret1.at[uz_, uy], ret1.at[uy_, uz]
        for d in (2, 1, 3, 0):
            to = (Y + d + (flip // 2) * uy) % 4
            ref = O.at[at * 8 + to]
            if d == 0 and flip // 2 == 0:

                @pl.when(c == 0)
                def _():
                    local(ref, to_y, y_done).start()

                @pl.when(c == 1)
                def _():
                    remote(ref, to_y, send.at[7], y_done, partner).start()
            else:
                remote(ref, to_y, send.at[7], y_done, dev(x, z, 2 * to + uy_, 0)).start()
            to = (Z + d + (flip % 2) * uz) % 4
            ref2 = O.at[at * 8 + 4 + to]
            if d == 0 and flip % 2 == 0:

                @pl.when(c == 1)
                def _():
                    local(ref2, to_z, z_done).start()

                @pl.when(c == 0)
                def _():
                    remote(ref2, to_z, send.at[7], z_done, partner).start()
            else:
                remote(ref2, to_z, send.at[7], z_done, dev(x, 2 * to + uz_, y, 1)).start()

    def back2(flip):
        b8 = jnp.where(c == 0, z, y)
        half, parity = b8 // 2, (b8 % 2) ^ flip
        for side in range(2):
            wait_bytes(O.at[pl.ds(0, 8)], ret1.at[parity, side])
        for d in (2, 1, 3, 0):
            to = (half + d + flip * (b8 % 2)) % 4
            ref = T2.at[parity * 4 + to]
            if d == 0 and flip == 0:
                local(ref, out.at[b8], ret2).start()
            else:
                far = 2 * to + parity
                yy = jnp.where(c == 0, y, far)
                zz = jnp.where(c == 0, far, z)
                remote(ref, out.at[b8], send.at[8], ret2, dev(x, zz, yy, c)).start()

    wait_bytes(tbl, tbl_sem)
    transform(0, 0)
    pl.semaphore_wait(barrier, 15)
    scatter_y(0)
    transform(0, 1)
    scatter_z(0)
    transform(1, 0)
    scatter_y(1)
    transform(1, 1)
    scatter_z(1)
    wait_bytes(weights, src_sem)
    scatter2(0)
    scatter2(1)
    settle(0)
    first_sends(0)
    settle(1)
    first_sends(1)
    core_send(u, A.at[c, u])
    rest_sends()
    first_arrive(0)
    x_arrive(u, 0, False)
    x_arrive(u, 1, True)
    first_arrive(1)
    pass_on(0, u)
    pass_on(1, u)
    for m in (my, mz, md):
        core_send(m, panel(m, u))
    x_arrive(my, 0, False)
    x_arrive(mz, 0, True)
    x_arrive(md, 0, False)
    wait_bytes(B.at[x, 0], own_sem.at[0])
    regroup(x, 0)
    n_arrive(0, my, True)
    n_arrive(1, mz, True)
    regroup(xl, 0)
    regroup(xr, 0)
    x_arrive(my, 1, True)
    n_arrive(0, md, True)
    n_arrive(1, md, True)
    x_arrive(mz, 1, False)
    wait_bytes(B.at[x, 1], own_sem.at[1])
    regroup(x, 1)
    x_arrive(md, 1, True)
    n_arrive(0, mz, False)
    n_arrive(1, my, False)
    regroup(xl, 1)
    regroup(xr, 1)
    x_far(0)
    regroup(xo, 0)
    x_far(1)
    regroup(xo, 1)
    multiply(0, 0)
    multiply(1, 2)
    d_arrive()
    multiply(2, 1)
    multiply(3, 3)
    back2(0)
    back2(1)
    wait_bytes(out, ret2)

    for h in range(2):
        wait_bytes(S.at[h, pl.ds(0, 7)], send.at[h])
        wait_bytes(T.at[h, pl.ds(0, 3)], send.at[2 + h])
    wait_bytes(B.at[pl.ds(0, 3)], send.at[4])
    wait_bytes(A.at[0, pl.ds(0, 3)], send.at[5])
    wait_bytes(A.at[0], send.at[6])
    wait_bytes(O.at[pl.ds(0, 30)], send.at[7])
    wait_bytes(T2.at[pl.ds(0, 7)], send.at[8])


def restore_kernel(spectra, table, out, held, tbl, result, load_sem, tbl_sem, sem):
    c = lax.axis_index("col") % 2
    loads = [pltpu.make_async_copy(spectra.at[:, :, core], held.at[core], load_sem.at[core]) for core in range(2)]
    loads[0].start()
    load_table = pltpu.make_async_copy(table, tbl, tbl_sem)
    load_table.start()
    loads[1].start()
    load_table.wait()
    copies = []
    for n in range(8):
        core, uy, uz = n // 4, (n // 2) % 2, n % 2
        if n % 4 == 0:
            loads[core].wait()
        tiles = []
        for j in range(16):
            y, z = 2 * (j // 4) + uy, 2 * (j % 4) + uz
            b, a = jnp.where(c == 0, z, y), jnp.where(c == 0, y, z)
            tiles.append(held[core, b, a])
        tiles = jnp.stack(tiles).astype(F32).reshape(16, 2, 8, 128)
        for h in range(2):
            left = tiles[:, h].reshape(128, 128).T.astype(BF16)
            traces = jnp.dot(left, tbl[...], preferred_element_type=F32).astype(BF16)
            for s in range(4):
                result[s, n * 256 + h * 128 : n * 256 + h * 128 + 128, :] = traces[:, s * 128 : s * 128 + 128]
        rows = pl.ds(n * 256, 256)
        copy = pltpu.make_async_copy(result.at[:, rows, :], out.at[:, rows, :], sem.at[n])
        copy.start()
        copies.append(copy)
    for copy in copies:
        copy.wait()


def on_device(forward, backward, traces, source_inverse):
    hbm = pl.BlockSpec(memory_space=pltpu.HBM)
    dma = pltpu.SemaphoreType.DMA
    width = traces.shape[1]
    spectra = pl.pallas_call(
        functools.partial(exchange_kernel, 1.0 / math.sqrt(width)),
        out_shape=jax.ShapeDtypeStruct((8, 8, 2, 16, 128), BF16),
        in_specs=[hbm, hbm, hbm],
        out_specs=hbm,
        scratch_shapes=[
            pltpu.VMEM((2, 4, 4, 2, 128, 128), BF16),
            pltpu.VMEM((128, 512), BF16),
            pltpu.SMEM((2, 16), F32),
            pltpu.VMEM((2, 8, 4, 2, 16, 128), BF16),
            pltpu.VMEM((2, 4, 4, 2, 2, 16, 128), BF16),
            pltpu.VMEM((2, 4, 4, 2, 2, 16, 128), BF16),
            pltpu.VMEM((2, 4, 256, 1024), BF16),
            pltpu.VMEM((4, 2, 4, 256, 128), BF16),
            pltpu.VMEM((4, 512, 512), BF16),
            pltpu.VMEM((32, 4, 16, 128), BF16),
            pltpu.VMEM((8, 8, 2, 16, 128), BF16),
            dma((2, 4)),
            dma(()),
            dma(()),
            dma((2,)),
            dma((2,)),
            dma((2, 2)),
            dma(()),
            dma((9,)),
            dma((3, 2, 4)),
            dma((2, 2)),
            dma((2, 4)),
            dma((2,)),
            dma((2, 4)),
            dma((4,)),
            dma((2,)),
        ],
        compiler_params=pltpu.CompilerParams(
            collective_id=0, has_side_effects=True, vmem_limit_bytes=VMEM_LIMIT
        ),
        name="exchange",
    )(traces.reshape(4, 8, 2, 128, 128), jnp.asarray(forward), source_inverse)
    return pl.pallas_call(
        restore_kernel,
        out_shape=jax.ShapeDtypeStruct(traces.shape, BF16),
        in_specs=[hbm, hbm],
        out_specs=hbm,
        scratch_shapes=[
            pltpu.VMEM((2, 8, 8, 16, 128), BF16),
            pltpu.VMEM((128, 512), BF16),
            pltpu.VMEM((4, width, 128), BF16),
            dma((2,)),
            dma(()),
            dma((8,)),
        ],
        compiler_params=pltpu.CompilerParams(vmem_limit_bytes=VMEM_LIMIT),
        name="restore",
    )(spectra, jnp.asarray(backward))


def solution(mesh):
    forward, backward = tables(16, 128)
    in_specs = (P(("freq", "row", "col"), None, None), P())
    out_specs = P(("freq", "row", "col"), None, None)
    return jax.shard_map(
        functools.partial(on_device, forward, backward),
        mesh=mesh,
        in_specs=in_specs,
        out_specs=out_specs,
        check_vma=False,
    )
```

```python
import functools
import math

import jax
import jax.numpy as jnp
import numpy as np
from jax import lax
from jax.experimental import pallas as pl
from jax.experimental.pallas import tpu as pltpu
from jax.sharding import PartitionSpec as P

MESH = pl.DeviceIdType.MESH
BF16 = jnp.bfloat16
F32 = jnp.float32
VMEM_LIMIT = 62 * 1024 * 1024 + 512 * 1024


def tables(count, length):
    bins = np.arange(count, dtype=np.int32) + 1
    times = np.arange(length, dtype=np.int32)
    index = bins[:, None] * times[None, :] % length
    angle = index.astype(np.float32) * np.float32(2.0 * math.pi / length)
    norm = np.float32(1.0 / math.sqrt(length))
    stacked = np.stack([np.cos(angle), -np.sin(angle)])
    forward = np.zeros((count, 2, 4, 4, length), np.float32)
    for i in range(4):
        forward[:, :, i, i] = np.transpose(stacked * norm, (1, 0, 2))
    forward = forward.reshape(count * 8, 4 * length)
    return forward.astype(jnp.bfloat16), (2 * forward).astype(jnp.bfloat16)


def low_rows(shape):
    return lax.broadcasted_iota(jnp.int32, shape, len(shape) - 2) < 4


def interleave(first, second):
    axis = first.ndim - 2
    low = low_rows(first.shape)
    top = jnp.where(low, first, pltpu.roll(second, 4, axis))
    bottom = jnp.where(low, pltpu.roll(first, 4, axis), second)
    return top, bottom


def exchange_kernel(
    scale,
    traces,
    table,
    source,
    out,
    tr,
    tbl,
    weights,
    S,
    T,
    R,
    A,
    B,
    W,
    acc,
    O,
    T2,
    tr_sem,
    tbl_sem,
    src_sem,
    in1,
    in2,
    ret1,
    ret2,
    send,
    x_sem,
    p_sem,
    n_sem,
    dp_sem,
    d_sem,
    core_sem,
    own_sem,
):
    x = lax.axis_index("freq")
    z = lax.axis_index("row")
    col = lax.axis_index("col")
    y = col // 2
    c = col % 2
    uy, uz = y % 2, z % 2
    Y, Z = y // 2, z // 2
    u = uy * 2 + uz

    def dev(xx, zz, yy, cc):
        return (xx, zz, yy * 2 + cc)

    def remote(src, dst, s, r, to):
        return pltpu.make_async_remote_copy(
            src_ref=src, dst_ref=dst, send_sem=s, recv_sem=r, device_id=to, device_id_type=MESH
        )

    def local(src, dst, s):
        return pltpu.make_async_copy(src, dst, s)

    def wait_bytes(ref, sem):
        pltpu.make_async_copy(ref, ref, sem).wait()

    near = uy

    def part(q):
        return q % 2, near if q < 2 else 1 - near

    def load(q):
        h, w = part(q)
        for core in range(2):
            k = core * 2 + w
            local(traces.at[:, pl.ds(2 * k, 2), h], tr.at[h, k], tr_sem.at[h, k]).start()

    barrier = pltpu.get_barrier_semaphore()
    partner = dev(x, z, y, 1 - c)
    left = dev((x + 3) % 4, z, y, c)
    right = dev((x + 1) % 4, z, y, c)
    yn = dev(x, z, y + 1 - 2 * uy, c)
    zn = dev(x, z + 1 - 2 * uz, y, c)
    dn = dev(x, z + 1 - 2 * uz, y + 1 - 2 * uy, c)
    others = []
    for d in (4, 2, 6):
        a_y, a_z = jnp.where(c == 0, (y + d) % 8, y), jnp.where(c == 0, z, (z + d) % 8)
        b_y, b_z = jnp.where(c == 0, y, (y + d) % 8), jnp.where(c == 0, (z + d) % 8, z)
        others += [dev(x, a_z, a_y, 0), dev(x, a_z, a_y, 1), dev(x, b_z, b_y, c)]
    others += [dn, left, right, yn, zn, partner]
    local(table, tbl, tbl_sem).start()
    load(0)
    for other in others:
        pl.semaphore_signal(barrier, inc=1, device_id=other, device_id_type=MESH)
    for q in range(1, 4):
        load(q)
    local(source, weights, src_sem).start()

    def transform(q, core):
        h, w = part(q)
        k = core * 2 + w
        wait_bytes(tr.at[h, k], tr_sem.at[h, k])
        block = jnp.concatenate([tr[h, k, s].reshape(256, 128) for s in range(4)], axis=1)
        data = lax.dot_general(tbl[...], block, (((1,), (1,)), ((), ())), preferred_element_type=F32)
        data = data.reshape(16, 8, 256)
        data = jnp.concatenate([data[:, :, :128], data[:, :, 128:]], axis=1)
        data = data.astype(BF16).reshape(4, 4, 16, 128)
        for first in range(4):
            if core == 0:
                S[q, first] = data[first]
            else:
                S[q, 4:8, first] = data[first]

    def scatter_y(q):
        for d in (2, 1, 3):
            to = (Y + d) % 4
            remote(S.at[q, to], T.at[q, :, Y, c], send.at[q], in1.at[q], dev(x, z, 2 * to + uy, 0)).start()

        @pl.when(c == 0)
        def _():
            local(S.at[q, Y], T.at[q, :, Y, c], in1.at[q]).start()

        @pl.when(c == 1)
        def _():
            remote(S.at[q, Y], T.at[q, :, Y, c], send.at[q], in1.at[q], partner).start()

    def scatter_z(q):
        for d in (2, 1, 3):
            to = (Z + d) % 4
            remote(S.at[q, 4 + to], T.at[q, :, Z, c], send.at[q], in1.at[q], dev(x, 2 * to + uz, y, 1)).start()

        @pl.when(c == 0)
        def _():
            remote(S.at[q, 4 + Z], T.at[q, :, Z, c], send.at[q], in1.at[q], partner).start()

        @pl.when(c == 1)
        def _():
            local(S.at[q, 4 + Z], T.at[q, :, Z, c], in1.at[q]).start()

    def scatter2(q):
        wait_bytes(T.at[q], in1.at[q])
        b4 = jnp.where(c == 0, Z, Y)
        for d in (2, 1, 3):
            to = (b4 + d) % 4
            far = 2 * to + jnp.where(c == 0, uz, uy)
            yy = jnp.where(c == 0, y, far)
            zz = jnp.where(c == 0, far, z)
            remote(T.at[q, to], R.at[q, b4], send.at[4 + q], in2.at[q], dev(x, zz, yy, c)).start()
        local(T.at[q, b4], R.at[q, b4], in2.at[q]).start()

    def settle(q):
        wait_bytes(R.at[q], in2.at[q])
        h, w = part(q)

        def step(n, carry):
            b, a = n // 4, n % 4
            row = pl.multiple_of(jnp.where(c == 0, a * 4 + b, n) * 16, 16)
            first = R[q, b, a, 0].astype(F32).reshape(2, 8, 128)
            second = R[q, b, a, 1].astype(F32).reshape(2, 8, 128)
            real, imag = interleave(first, second)
            for v in range(2):
                tile = jnp.concatenate([real[v], imag[v]], axis=0).astype(BF16)
                A[c, u, pl.ds(row, 16), pl.ds(pl.multiple_of((2 * w + v) * 256 + h * 128, 128), 128)] = tile
            return carry

        lax.fori_loop(0, 16, step, 0, unroll=4)

    my, mz, md = u ^ 2, u ^ 1, u ^ 3
    xl, xr, xo = (x + 3) % 4, (x + 1) % 4, (x + 2) % 4

    def lanes(v, h):
        return pl.ds(pl.multiple_of(v * 256 + h * 128, 128), 128)

    def panel(m, v, rows=pl.ds(0, 256)):
        return A.at[c, m, rows, pl.ds(pl.multiple_of(v * 256, 256), 256)]

    def x_send(m, h):
        ref = A.at[c, m, :, lanes(u, h)]
        remote(ref, B.at[x, h, m], send.at[8], x_sem.at[0, h, m], right).start()
        remote(ref, B.at[x, h, m], send.at[8], x_sem.at[1, h, m], left).start()

    def core_send(m, ref):
        remote(ref, ref, send.at[10], core_sem.at[m], partner).start()

    def first_send(which, h):
        v, sem, to = ((my, p_sem.at[0, h], yn), (mz, p_sem.at[1, h], zn), (md, dp_sem.at[h], dn))[which]
        ref = A.at[c, u, :, lanes(v, h)]
        remote(ref, ref, send.at[9], sem, to).start()

    def first_arrive(which, h):
        m, sem = ((my, p_sem.at[0, h]), (mz, p_sem.at[1, h]), (md, dp_sem.at[h]))[which]
        wait_bytes(A.at[c, m, :, lanes(u, h)], sem)
        x_send(m, h)

    def own_copy(h):
        return local(A.at[c, :, :, lanes(u, h)], B.at[x, h], own_sem.at[h])

    def rest_sends():
        for v0, v1 in ((u, u), (mz, my), (md, md)):
            remote(panel(u, v0), panel(u, v0), send.at[9], n_sem.at[0, v0], yn).start()
            remote(panel(u, v1), panel(u, v1), send.at[9], n_sem.at[1, v1], zn).start()

    def pass_on(which, v):
        m = (my, mz)[which]
        half = panel(m, v, pl.ds(which * 128, 128))
        remote(half, half, send.at[9], d_sem.at[which, v], (zn, yn)[which]).start()

    def n_arrive(which, v, forward):
        m = (my, mz)[which]
        wait_bytes(panel(m, v), n_sem.at[which, v])
        if forward:
            pass_on(which, v)
        core_send(m, panel(m, v))

    def x_arrive(m, h, odd):
        wait_bytes(B.at[xl, h, m], x_sem.at[0, h, m])
        if not odd:
            remote(B.at[xl, h, m], B.at[xl, h, m], send.at[8], x_sem.at[2, h, m], right).start()
        wait_bytes(B.at[xr, h, m], x_sem.at[1, h, m])
        if odd:
            remote(B.at[xr, h, m], B.at[xr, h, m], send.at[8], x_sem.at[2, h, m], left).start()

    def x_far(h):
        for m in (u, my, mz, md):
            wait_bytes(B.at[xo, h, m], x_sem.at[2, h, m])

    def d_arrive():
        for v0, v1 in ((mz, my), (md, md), (my, mz)):
            for which, v in ((0, v0), (1, v1)):
                half = panel(md, v, pl.ds(which * 128, 128))
                wait_bytes(half, d_sem.at[which, v])
                core_send(md, half)

    def regroup(xp, h):
        def step(n, carry):
            uz_, Z_, Y_ = n // 16, (n // 4) % 4, n % 4
            row = pl.multiple_of((Y_ * 4 + Z_) * 16, 16)
            even = B[xp, h, uz_, pl.ds(row, 16), :].astype(F32)
            odd = B[xp, h, 2 + uz_, pl.ds(row, 16), :].astype(F32)
            at = pl.ds(pl.multiple_of((2 * Z_ + uz_) * 64 + Y_ * 16, 16), 16)
            W[xp, at, h * 128 : h * 128 + 128] = jnp.concatenate([even[:8], odd[:8]], axis=0).astype(BF16)
            W[xp, at, 256 + h * 128 : 384 + h * 128] = jnp.concatenate([even[8:], odd[8:]], axis=0).astype(BF16)
            return carry

        lax.fori_loop(0, 32, step, 0, unroll=8)

    j = Y * 4 + Z

    def term(m, xp):
        left = A[xp // 2, m, :, pl.ds(pl.multiple_of((xp % 2) * 512, 512), 512)]
        return jnp.dot(left, W[xp], preferred_element_type=F32)

    def multiply(at, flip):
        m = u ^ flip
        w_real, w_imag = weights[0, j], weights[1, j]
        if flip == 0:
            total = acc[...] + term(m, xo)
        else:
            wait_bytes(A.at[1 - c, m], core_sem.at[m])
            total = jnp.dot(A[0, m], W[0:2].reshape(1024, 512), preferred_element_type=F32)
            total += jnp.dot(A[1, m], W[2:4].reshape(1024, 512), preferred_element_type=F32)
        total = total.reshape(16, 2, 8, 512)
        real = total[:, 0, :, :256] - total[:, 1, :, 256:]
        imag = total[:, 0, :, 256:] + total[:, 1, :, :256]
        pred_real = (w_real * real - w_imag * imag) * scale
        pred_imag = (w_real * imag + w_imag * real) * scale
        for core, part in enumerate(interleave(pred_real, pred_imag)):
            part = jnp.concatenate([part[:, :, :128], part[:, :, 128:]], axis=1).astype(BF16)
            part = part.reshape(4, 4, 16, 128)
            for first in range(4):
                if core == 0:
                    O[at * 8 + first] = part[first]
                else:
                    O[at * 8 + 4 : at * 8 + 8, first] = part[first]

        uy_, uz_ = uy ^ (flip // 2), uz ^ (flip % 2)
        to_y = T2.at[pl.ds(uz_ * 4, 4), uy, Y, c]
        to_z = T2.at[pl.ds(uy_ * 4, 4), uz, Z, c]
        y_done, z_done = ret1.at[uz_, uy], ret1.at[uy_, uz]
        for d in (2, 1, 3, 0):
            to = (Y + d + (flip // 2) * uy) % 4
            ref = O.at[at * 8 + to]
            if d == 0 and flip // 2 == 0:

                @pl.when(c == 0)
                def _():
                    local(ref, to_y, y_done).start()

                @pl.when(c == 1)
                def _():
                    remote(ref, to_y, send.at[11], y_done, partner).start()
            else:
                remote(ref, to_y, send.at[11], y_done, dev(x, z, 2 * to + uy_, 0)).start()
            to = (Z + d + (flip % 2) * uz) % 4
            ref2 = O.at[at * 8 + 4 + to]
            if d == 0 and flip % 2 == 0:

                @pl.when(c == 1)
                def _():
                    local(ref2, to_z, z_done).start()

                @pl.when(c == 0)
                def _():
                    remote(ref2, to_z, send.at[11], z_done, partner).start()
            else:
                remote(ref2, to_z, send.at[11], z_done, dev(x, 2 * to + uz_, y, 1)).start()

    def back2(flip):
        b8, own = jnp.where(c == 0, z, y), jnp.where(c == 0, uz, uy)
        differ = jnp.where(c == 0, flip % 2, flip // 2)
        parity = own ^ differ
        side = jnp.where(c == 0, uy ^ (flip // 2), uz ^ (flip % 2))
        wait_bytes(O.at[pl.ds(0, 8)], ret1.at[parity, side])
        for d in (2, 1, 3, 0):
            to = (b8 // 2 + d + differ * own) % 4
            ref = T2.at[parity * 4 + to, side]
            far = 2 * to + parity
            yy = jnp.where(c == 0, y, far)
            zz = jnp.where(c == 0, far, z)
            if d == 0 and flip != 3:

                @pl.when(differ == 0)
                def _():
                    local(ref, out.at[b8, side], ret2).start()

                @pl.when(differ != 0)
                def _():
                    remote(ref, out.at[b8, side], send.at[12], ret2, dev(x, zz, yy, c)).start()
            else:
                remote(ref, out.at[b8, side], send.at[12], ret2, dev(x, zz, yy, c)).start()

    wait_bytes(tbl, tbl_sem)
    for q in range(4):
        transform(q, 0)
        if q == 0:
            pl.semaphore_wait(barrier, 15)
        scatter_y(q)
        transform(q, 1)
        scatter_z(q)
    wait_bytes(weights, src_sem)
    for q in range(4):
        scatter2(q)
    settle(0)
    x_send(u, 0)
    first_send(1, 0)
    settle(1)
    x_send(u, 1)
    first_send(1, 1)
    settle(2)
    first_send(0, 0)
    first_send(2, 0)
    settle(3)
    first_send(0, 1)
    first_send(2, 1)
    core_send(u, A.at[c, u])
    rest_sends()
    first_arrive(1, 0)
    first_arrive(1, 1)
    x_arrive(u, 0, False)
    x_arrive(u, 1, True)
    pass_on(1, u)
    first_arrive(0, 0)
    first_arrive(2, 0)
    own_copy(0).start()
    first_arrive(0, 1)
    first_arrive(2, 1)
    own_copy(1).start()
    pass_on(0, u)
    for m in (my, mz, md):
        core_send(m, panel(m, u))
    x_arrive(mz, 0, False)
    x_arrive(mz, 1, True)
    x_arrive(my, 0, False)
    x_arrive(md, 0, True)
    wait_bytes(B.at[x, 0], own_sem.at[0])
    regroup(x, 0)
    n_arrive(0, my, True)
    n_arrive(1, mz, True)
    regroup(xl, 0)
    regroup(xr, 0)
    x_arrive(my, 1, False)
    n_arrive(0, md, True)
    n_arrive(1, md, True)
    x_arrive(md, 1, True)
    wait_bytes(B.at[x, 1], own_sem.at[1])
    regroup(x, 1)
    n_arrive(0, mz, False)
    n_arrive(1, my, False)
    regroup(xl, 1)
    regroup(xr, 1)
    wait_bytes(A.at[1 - c, u], core_sem.at[u])
    acc[...] = term(u, x)
    acc[...] += term(u, xl)
    acc[...] += term(u, xr)
    x_far(0)
    regroup(xo, 0)
    x_far(1)
    regroup(xo, 1)
    multiply(0, 0)
    multiply(1, 2)
    d_arrive()
    multiply(2, 1)
    multiply(3, 3)
    for flip in (0, 2, 1, 3):
        back2(flip)
    wait_bytes(out, ret2)

    for q in range(4):
        wait_bytes(S.at[q, pl.ds(0, 7)], send.at[q])
        wait_bytes(T.at[q, pl.ds(0, 3)], send.at[4 + q])
    wait_bytes(B.at[pl.ds(0, 3)], send.at[8])
    wait_bytes(A.at[0, pl.ds(0, 3)], send.at[9])
    wait_bytes(A.at[0], send.at[10])
    wait_bytes(O.at[pl.ds(0, 30)], send.at[11])
    wait_bytes(T2.at[pl.ds(0, 7)], send.at[12])


def restore_kernel(spectra, table, out, held, tbl, result, load_sem, tbl_sem, sem):
    c = lax.axis_index("col") % 2
    loads = [pltpu.make_async_copy(spectra.at[:, :, :, core], held.at[core], load_sem.at[core]) for core in range(2)]
    loads[0].start()
    load_table = pltpu.make_async_copy(table, tbl, tbl_sem)
    load_table.start()
    loads[1].start()
    load_table.wait()
    copies = []
    for n in range(8):
        core, uy, uz = n // 4, (n // 2) % 2, n % 2
        if n % 4 == 0:
            loads[core].wait()
        tiles = []
        for j in range(16):
            y, z = 2 * (j // 4) + uy, 2 * (j % 4) + uz
            b, a = jnp.where(c == 0, z, y), jnp.where(c == 0, y, z)
            tiles.append(held[core, b, a % 2, a // 2])
        tiles = jnp.stack(tiles).astype(F32).reshape(16, 2, 8, 128)
        for h in range(2):
            left = tiles[:, h].reshape(128, 128).T.astype(BF16)
            traces = jnp.dot(left, tbl[...], preferred_element_type=F32).astype(BF16)
            for s in range(4):
                result[s, n * 256 + h * 128 : n * 256 + h * 128 + 128, :] = traces[:, s * 128 : s * 128 + 128]
        rows = pl.ds(n * 256, 256)
        copy = pltpu.make_async_copy(result.at[:, rows, :], out.at[:, rows, :], sem.at[n])
        copy.start()
        copies.append(copy)
    for copy in copies:
        copy.wait()


def on_device(forward, backward, traces, source_inverse):
    hbm = pl.BlockSpec(memory_space=pltpu.HBM)
    dma = pltpu.SemaphoreType.DMA
    width = traces.shape[1]
    spectra = pl.pallas_call(
        functools.partial(exchange_kernel, 1.0 / math.sqrt(width)),
        out_shape=jax.ShapeDtypeStruct((8, 2, 4, 2, 16, 128), BF16),
        in_specs=[hbm, hbm, hbm],
        out_specs=hbm,
        scratch_shapes=[
            pltpu.VMEM((2, 4, 4, 2, 128, 128), BF16),
            pltpu.VMEM((128, 512), BF16),
            pltpu.SMEM((2, 16), F32),
            pltpu.VMEM((4, 8, 4, 16, 128), BF16),
            pltpu.VMEM((4, 4, 4, 2, 16, 128), BF16),
            pltpu.VMEM((4, 4, 4, 2, 16, 128), BF16),
            pltpu.VMEM((2, 4, 256, 1024), BF16),
            pltpu.VMEM((4, 2, 4, 256, 128), BF16),
            pltpu.VMEM((4, 512, 512), BF16),
            pltpu.VMEM((256, 512), F32),
            pltpu.VMEM((32, 4, 16, 128), BF16),
            pltpu.VMEM((8, 2, 4, 2, 16, 128), BF16),
            dma((2, 4)),
            dma(()),
            dma(()),
            dma((4,)),
            dma((4,)),
            dma((2, 2)),
            dma(()),
            dma((13,)),
            dma((3, 2, 4)),
            dma((2, 2)),
            dma((2, 4)),
            dma((2,)),
            dma((2, 4)),
            dma((4,)),
            dma((2,)),
        ],
        compiler_params=pltpu.CompilerParams(
            collective_id=0, has_side_effects=True, vmem_limit_bytes=VMEM_LIMIT
        ),
        name="exchange",
    )(traces.reshape(4, 8, 2, 128, 128), jnp.asarray(forward), source_inverse)
    return pl.pallas_call(
        restore_kernel,
        out_shape=jax.ShapeDtypeStruct(traces.shape, BF16),
        in_specs=[hbm, hbm],
        out_specs=hbm,
        scratch_shapes=[
            pltpu.VMEM((2, 8, 2, 4, 16, 128), BF16),
            pltpu.VMEM((128, 512), BF16),
            pltpu.VMEM((4, width, 128), BF16),
            dma((2,)),
            dma(()),
            dma((8,)),
        ],
        compiler_params=pltpu.CompilerParams(vmem_limit_bytes=VMEM_LIMIT),
        name="restore",
    )(spectra, jnp.asarray(backward))


def solution(mesh):
    forward, backward = tables(16, 128)
    in_specs = (P(("freq", "row", "col"), None, None), P())
    out_specs = P(("freq", "row", "col"), None, None)
    return jax.shard_map(
        functools.partial(on_device, forward, backward),
        mesh=mesh,
        in_specs=in_specs,
        out_specs=out_specs,
        check_vma=False,
    )
```

```python
import functools
import math

import jax
import jax.numpy as jnp
import numpy as np
from jax import lax
from jax.experimental import pallas as pl
from jax.experimental.pallas import tpu as pltpu
from jax.sharding import PartitionSpec as P

MESH = pl.DeviceIdType.MESH
BF16 = jnp.bfloat16
F32 = jnp.float32
VMEM_LIMIT = 62 * 1024 * 1024 + 512 * 1024


def tables(count, length):
    bins = np.arange(count, dtype=np.int32) + 1
    times = np.arange(length, dtype=np.int32)
    index = bins[:, None] * times[None, :] % length
    angle = index.astype(np.float32) * np.float32(2.0 * math.pi / length)
    norm = np.float32(1.0 / math.sqrt(length))
    stacked = np.stack([np.cos(angle), -np.sin(angle)])
    forward = np.zeros((count, 2, 4, 4, length), np.float32)
    for i in range(4):
        forward[:, :, i, i] = np.transpose(stacked * norm, (1, 0, 2))
    forward = forward.reshape(count * 8, 4 * length)
    return forward.astype(jnp.bfloat16), (2 * forward).astype(jnp.bfloat16)


def low_rows(shape):
    return lax.broadcasted_iota(jnp.int32, shape, len(shape) - 2) < 4


def interleave(first, second):
    axis = first.ndim - 2
    low = low_rows(first.shape)
    top = jnp.where(low, first, pltpu.roll(second, 4, axis))
    bottom = jnp.where(low, pltpu.roll(first, 4, axis), second)
    return top, bottom


def exchange_kernel(
    scale,
    traces,
    table,
    source,
    out,
    tr,
    tbl,
    weights,
    S,
    T,
    R,
    A,
    B,
    W,
    acc,
    O,
    T2,
    tr_sem,
    tbl_sem,
    src_sem,
    in1,
    in2,
    ret1,
    ret2,
    send,
    x_sem,
    p_sem,
    n_sem,
    dp_sem,
    d_sem,
    core_sem,
    own_sem,
):
    x = lax.axis_index("freq")
    z = lax.axis_index("row")
    col = lax.axis_index("col")
    y = col // 2
    c = col % 2
    uy, uz = y % 2, z % 2
    Y, Z = y // 2, z // 2
    u = uy * 2 + uz

    def dev(xx, zz, yy, cc):
        return (xx, zz, yy * 2 + cc)

    def remote(src, dst, s, r, to):
        return pltpu.make_async_remote_copy(
            src_ref=src, dst_ref=dst, send_sem=s, recv_sem=r, device_id=to, device_id_type=MESH
        )

    def local(src, dst, s):
        return pltpu.make_async_copy(src, dst, s)

    def wait_bytes(ref, sem):
        pltpu.make_async_copy(ref, ref, sem).wait()

    near = uy

    def part(q):
        return q % 2, near if q < 2 else 1 - near

    def load(q):
        h, w = part(q)
        for core in range(2):
            k = core * 2 + w
            local(traces.at[:, pl.ds(2 * k, 2), h], tr.at[h, k], tr_sem.at[h, k]).start()

    barrier = pltpu.get_barrier_semaphore()
    partner = dev(x, z, y, 1 - c)
    left = dev((x + 3) % 4, z, y, c)
    right = dev((x + 1) % 4, z, y, c)
    yn = dev(x, z, y + 1 - 2 * uy, c)
    zn = dev(x, z + 1 - 2 * uz, y, c)
    dn = dev(x, z + 1 - 2 * uz, y + 1 - 2 * uy, c)
    others = []
    for d in (4, 2, 6):
        a_y, a_z = jnp.where(c == 0, (y + d) % 8, y), jnp.where(c == 0, z, (z + d) % 8)
        b_y, b_z = jnp.where(c == 0, y, (y + d) % 8), jnp.where(c == 0, (z + d) % 8, z)
        others += [dev(x, a_z, a_y, 0), dev(x, a_z, a_y, 1), dev(x, b_z, b_y, c)]
    others += [dn, left, right, yn, zn, partner]
    local(table, tbl, tbl_sem).start()
    load(0)
    for other in others:
        pl.semaphore_signal(barrier, inc=1, device_id=other, device_id_type=MESH)
    for q in range(1, 4):
        load(q)
    local(source, weights, src_sem).start()

    def transform(q, core):
        h, w = part(q)
        k = core * 2 + w
        wait_bytes(tr.at[h, k], tr_sem.at[h, k])
        block = jnp.concatenate([tr[h, k, s].reshape(256, 128) for s in range(4)], axis=1)
        data = lax.dot_general(tbl[...], block, (((1,), (1,)), ((), ())), preferred_element_type=F32)
        data = data.reshape(16, 8, 256)
        data = jnp.concatenate([data[:, :, :128], data[:, :, 128:]], axis=1)
        data = data.astype(BF16).reshape(4, 4, 16, 128)
        for first in range(4):
            if core == 0:
                S[q, first] = data[first]
            else:
                S[q, 4:8, first] = data[first]

    def scatter_y(q):
        for d in (2, 1, 3):
            to = (Y + d) % 4
            remote(S.at[q, to], T.at[q, :, Y, c], send.at[q], in1.at[q], dev(x, z, 2 * to + uy, 0)).start()

        @pl.when(c == 0)
        def _():
            local(S.at[q, Y], T.at[q, :, Y, c], in1.at[q]).start()

        @pl.when(c == 1)
        def _():
            remote(S.at[q, Y], T.at[q, :, Y, c], send.at[q], in1.at[q], partner).start()

    def scatter_z(q):
        for d in (2, 1, 3):
            to = (Z + d) % 4
            remote(S.at[q, 4 + to], T.at[q, :, Z, c], send.at[q], in1.at[q], dev(x, 2 * to + uz, y, 1)).start()

        @pl.when(c == 0)
        def _():
            remote(S.at[q, 4 + Z], T.at[q, :, Z, c], send.at[q], in1.at[q], partner).start()

        @pl.when(c == 1)
        def _():
            local(S.at[q, 4 + Z], T.at[q, :, Z, c], in1.at[q]).start()

    def scatter2(q):
        wait_bytes(T.at[q], in1.at[q])
        b4 = jnp.where(c == 0, Z, Y)
        for d in (2, 1, 3):
            to = (b4 + d) % 4
            far = 2 * to + jnp.where(c == 0, uz, uy)
            yy = jnp.where(c == 0, y, far)
            zz = jnp.where(c == 0, far, z)
            remote(T.at[q, to], R.at[q, b4], send.at[4 + q], in2.at[q], dev(x, zz, yy, c)).start()
        local(T.at[q, b4], R.at[q, b4], in2.at[q]).start()

    def settle(q):
        wait_bytes(R.at[q], in2.at[q])
        h, w = part(q)

        def step(n, carry):
            b, a = n // 4, n % 4
            row = pl.multiple_of(jnp.where(c == 0, a * 4 + b, n) * 16, 16)
            first = R[q, b, a, 0].astype(F32).reshape(2, 8, 128)
            second = R[q, b, a, 1].astype(F32).reshape(2, 8, 128)
            real, imag = interleave(first, second)
            for v in range(2):
                tile = jnp.concatenate([real[v], imag[v]], axis=0).astype(BF16)
                A[c, u, pl.ds(row, 16), pl.ds(pl.multiple_of((2 * w + v) * 256 + h * 128, 128), 128)] = tile
            return carry

        lax.fori_loop(0, 16, step, 0, unroll=4)

    my, mz, md = u ^ 2, u ^ 1, u ^ 3
    xl, xr, xo = (x + 3) % 4, (x + 1) % 4, (x + 2) % 4

    def lanes(v, h):
        return pl.ds(pl.multiple_of(v * 256 + h * 128, 128), 128)

    def panel(m, v, rows=pl.ds(0, 256)):
        return A.at[c, m, rows, pl.ds(pl.multiple_of(v * 256, 256), 256)]

    def x_send(m, h):
        ref = A.at[c, m, :, lanes(u, h)]
        remote(ref, B.at[x, h, m], send.at[8], x_sem.at[0, h, m], right).start()
        remote(ref, B.at[x, h, m], send.at[8], x_sem.at[1, h, m], left).start()

    def core_send(m, ref):
        remote(ref, ref, send.at[10], core_sem.at[m], partner).start()

    def first_send(which, h):
        v, sem, to = ((my, p_sem.at[0, h], yn), (mz, p_sem.at[1, h], zn), (md, dp_sem.at[h], dn))[which]
        ref = A.at[c, u, :, lanes(v, h)]
        remote(ref, ref, send.at[9], sem, to).start()

    def first_arrive(which, h):
        m, sem = ((my, p_sem.at[0, h]), (mz, p_sem.at[1, h]), (md, dp_sem.at[h]))[which]
        wait_bytes(A.at[c, m, :, lanes(u, h)], sem)
        x_send(m, h)

    def own_copy(h):
        return local(A.at[c, :, :, lanes(u, h)], B.at[x, h], own_sem.at[h])

    def rest_sends():
        for v0, v1 in ((u, u), (mz, my), (md, md)):
            remote(panel(u, v0), panel(u, v0), send.at[9], n_sem.at[0, v0], yn).start()
            remote(panel(u, v1), panel(u, v1), send.at[9], n_sem.at[1, v1], zn).start()

    def pass_on(which, v):
        m = (my, mz)[which]
        half = panel(m, v, pl.ds(which * 128, 128))
        remote(half, half, send.at[9], d_sem.at[which, v], (zn, yn)[which]).start()

    def n_arrive(which, v, forward):
        m = (my, mz)[which]
        wait_bytes(panel(m, v), n_sem.at[which, v])
        if forward:
            pass_on(which, v)
        core_send(m, panel(m, v))

    def x_arrive(m, h, odd):
        wait_bytes(B.at[xl, h, m], x_sem.at[0, h, m])
        if not odd:
            remote(B.at[xl, h, m], B.at[xl, h, m], send.at[8], x_sem.at[2, h, m], right).start()
        wait_bytes(B.at[xr, h, m], x_sem.at[1, h, m])
        if odd:
            remote(B.at[xr, h, m], B.at[xr, h, m], send.at[8], x_sem.at[2, h, m], left).start()

    def x_arrive_last(m, h):
        for side, (src, to) in enumerate(((xl, right), (xr, left))):
            wait_bytes(B.at[src, h, m], x_sem.at[side, h, m])
            half = B.at[src, h, m, pl.ds(side * 128, 128), :]
            remote(half, half, send.at[8], x_sem.at[2, h, m], to).start()

    def x_far(h):
        for m in (u, my, mz, md):
            wait_bytes(B.at[xo, h, m], x_sem.at[2, h, m])

    def d_arrive():
        for v0, v1 in ((mz, my), (md, md), (my, mz)):
            for which, v in ((0, v0), (1, v1)):
                half = panel(md, v, pl.ds(which * 128, 128))
                wait_bytes(half, d_sem.at[which, v])
                core_send(md, half)

    def regroup(xp, h):
        def step(n, carry):
            uz_, Z_, Y_ = n // 16, (n // 4) % 4, n % 4
            row = pl.multiple_of((Y_ * 4 + Z_) * 16, 16)
            even = B[xp, h, uz_, pl.ds(row, 16), :].astype(F32)
            odd = B[xp, h, 2 + uz_, pl.ds(row, 16), :].astype(F32)
            at = pl.ds(pl.multiple_of((2 * Z_ + uz_) * 64 + Y_ * 16, 16), 16)
            W[xp, at, h * 128 : h * 128 + 128] = jnp.concatenate([even[:8], odd[:8]], axis=0).astype(BF16)
            W[xp, at, 256 + h * 128 : 384 + h * 128] = jnp.concatenate([even[8:], odd[8:]], axis=0).astype(BF16)
            return carry

        lax.fori_loop(0, 32, step, 0, unroll=8)

    j = Y * 4 + Z

    def term(m, xp):
        left = A[xp // 2, m, :, pl.ds(pl.multiple_of((xp % 2) * 512, 512), 512)]
        return jnp.dot(left, W[xp], preferred_element_type=F32)

    def multiply(at, flip):
        m = u ^ flip
        w_real, w_imag = weights[0, j], weights[1, j]
        if flip == 0:
            total = acc[...] + term(m, xo)
        else:
            wait_bytes(A.at[1 - c, m], core_sem.at[m])
            total = jnp.dot(A[0, m], W[0:2].reshape(1024, 512), preferred_element_type=F32)
            total += jnp.dot(A[1, m], W[2:4].reshape(1024, 512), preferred_element_type=F32)
        total = total.reshape(16, 2, 8, 512)
        real = total[:, 0, :, :256] - total[:, 1, :, 256:]
        imag = total[:, 0, :, 256:] + total[:, 1, :, :256]
        pred_real = (w_real * real - w_imag * imag) * scale
        pred_imag = (w_real * imag + w_imag * real) * scale
        for core, part in enumerate(interleave(pred_real, pred_imag)):
            part = jnp.concatenate([part[:, :, :128], part[:, :, 128:]], axis=1).astype(BF16)
            part = part.reshape(4, 4, 16, 128)
            for first in range(4):
                if core == 0:
                    O[at * 8 + first] = part[first]
                else:
                    O[at * 8 + 4 : at * 8 + 8, first] = part[first]

        uy_, uz_ = uy ^ (flip // 2), uz ^ (flip % 2)
        to_y = T2.at[pl.ds(uz_ * 4, 4), uy, Y, c]
        to_z = T2.at[pl.ds(uy_ * 4, 4), uz, Z, c]
        y_done, z_done = ret1.at[uz_, uy], ret1.at[uy_, uz]
        for d in (2, 1, 3, 0):
            to = (Y + d + (flip // 2) * uy) % 4
            ref = O.at[at * 8 + to]
            if d == 0 and flip // 2 == 0:

                @pl.when(c == 0)
                def _():
                    local(ref, to_y, y_done).start()

                @pl.when(c == 1)
                def _():
                    remote(ref, to_y, send.at[11], y_done, partner).start()
            else:
                remote(ref, to_y, send.at[11], y_done, dev(x, z, 2 * to + uy_, 0)).start()
            to = (Z + d + (flip % 2) * uz) % 4
            ref2 = O.at[at * 8 + 4 + to]
            if d == 0 and flip % 2 == 0:

                @pl.when(c == 1)
                def _():
                    local(ref2, to_z, z_done).start()

                @pl.when(c == 0)
                def _():
                    remote(ref2, to_z, send.at[11], z_done, partner).start()
            else:
                remote(ref2, to_z, send.at[11], z_done, dev(x, 2 * to + uz_, y, 1)).start()

    def back2(flip):
        b8, own = jnp.where(c == 0, z, y), jnp.where(c == 0, uz, uy)
        differ = jnp.where(c == 0, flip % 2, flip // 2)
        parity = own ^ differ
        side = jnp.where(c == 0, uy ^ (flip // 2), uz ^ (flip % 2))
        wait_bytes(O.at[pl.ds(0, 8)], ret1.at[parity, side])
        for d in (2, 1, 3, 0):
            to = (b8 // 2 + d + differ * own) % 4
            ref = T2.at[parity * 4 + to, side]
            far = 2 * to + parity
            yy = jnp.where(c == 0, y, far)
            zz = jnp.where(c == 0, far, z)
            if d == 0 and flip != 3:

                @pl.when(differ == 0)
                def _():
                    local(ref, out.at[b8, side], ret2).start()

                @pl.when(differ != 0)
                def _():
                    remote(ref, out.at[b8, side], send.at[12], ret2, dev(x, zz, yy, c)).start()
            else:
                remote(ref, out.at[b8, side], send.at[12], ret2, dev(x, zz, yy, c)).start()

    wait_bytes(tbl, tbl_sem)
    for q in range(4):
        transform(q, 0)
        if q == 0:
            pl.semaphore_wait(barrier, 15)
        scatter_y(q)
        transform(q, 1)
        scatter_z(q)
    wait_bytes(weights, src_sem)
    for q in range(4):
        scatter2(q)
    settle(0)
    x_send(u, 0)
    first_send(1, 0)
    settle(1)
    x_send(u, 1)
    first_send(1, 1)
    settle(2)
    first_send(0, 0)
    first_send(2, 0)
    settle(3)
    first_send(0, 1)
    first_send(2, 1)
    core_send(u, A.at[c, u])
    rest_sends()
    first_arrive(1, 0)
    first_arrive(1, 1)
    x_arrive(u, 0, False)
    x_arrive(u, 1, True)
    pass_on(1, u)
    first_arrive(0, 0)
    first_arrive(2, 0)
    own_copy(0).start()
    first_arrive(0, 1)
    first_arrive(2, 1)
    own_copy(1).start()
    pass_on(0, u)
    for m in (my, mz, md):
        core_send(m, panel(m, u))
    x_arrive(mz, 0, False)
    x_arrive(mz, 1, True)
    x_arrive(my, 0, False)
    x_arrive(md, 0, True)
    wait_bytes(B.at[x, 0], own_sem.at[0])
    regroup(x, 0)
    n_arrive(0, my, True)
    n_arrive(1, mz, True)
    x_arrive_last(my, 1)
    n_arrive(0, md, True)
    n_arrive(1, md, True)
    x_arrive_last(md, 1)
    regroup(xl, 0)
    regroup(xr, 0)
    wait_bytes(B.at[x, 1], own_sem.at[1])
    regroup(x, 1)
    n_arrive(0, mz, False)
    n_arrive(1, my, False)
    regroup(xl, 1)
    regroup(xr, 1)
    wait_bytes(A.at[1 - c, u], core_sem.at[u])
    acc[...] = term(u, x)
    acc[...] += term(u, xl)
    acc[...] += term(u, xr)
    x_far(0)
    regroup(xo, 0)
    x_far(1)
    regroup(xo, 1)
    multiply(0, 0)
    multiply(1, 2)
    d_arrive()
    multiply(2, 1)
    multiply(3, 3)
    for flip in (0, 2, 1, 3):
        back2(flip)
    wait_bytes(out, ret2)

    for q in range(4):
        wait_bytes(S.at[q, pl.ds(0, 7)], send.at[q])
        wait_bytes(T.at[q, pl.ds(0, 3)], send.at[4 + q])
    wait_bytes(B.at[pl.ds(0, 3)], send.at[8])
    wait_bytes(A.at[0, pl.ds(0, 3)], send.at[9])
    wait_bytes(A.at[0], send.at[10])
    wait_bytes(O.at[pl.ds(0, 30)], send.at[11])
    wait_bytes(T2.at[pl.ds(0, 7)], send.at[12])


def restore_kernel(spectra, table, out, held, tbl, result, load_sem, tbl_sem, sem):
    c = lax.axis_index("col") % 2
    loads = [pltpu.make_async_copy(spectra.at[:, :, :, core], held.at[core], load_sem.at[core]) for core in range(2)]
    loads[0].start()
    load_table = pltpu.make_async_copy(table, tbl, tbl_sem)
    load_table.start()
    loads[1].start()
    load_table.wait()
    copies = []
    for n in range(8):
        core, uy, uz = n // 4, (n // 2) % 2, n % 2
        if n % 4 == 0:
            loads[core].wait()
        tiles = []
        for j in range(16):
            y, z = 2 * (j // 4) + uy, 2 * (j % 4) + uz
            b, a = jnp.where(c == 0, z, y), jnp.where(c == 0, y, z)
            tiles.append(held[core, b, a % 2, a // 2])
        tiles = jnp.stack(tiles).astype(F32).reshape(16, 2, 8, 128)
        for h in range(2):
            left = tiles[:, h].reshape(128, 128).T.astype(BF16)
            traces = jnp.dot(left, tbl[...], preferred_element_type=F32).astype(BF16)
            for s in range(4):
                result[s, n * 256 + h * 128 : n * 256 + h * 128 + 128, :] = traces[:, s * 128 : s * 128 + 128]
        rows = pl.ds(n * 256, 256)
        copy = pltpu.make_async_copy(result.at[:, rows, :], out.at[:, rows, :], sem.at[n])
        copy.start()
        copies.append(copy)
    for copy in copies:
        copy.wait()


def on_device(forward, backward, traces, source_inverse):
    hbm = pl.BlockSpec(memory_space=pltpu.HBM)
    dma = pltpu.SemaphoreType.DMA
    width = traces.shape[1]
    spectra = pl.pallas_call(
        functools.partial(exchange_kernel, 1.0 / math.sqrt(width)),
        out_shape=jax.ShapeDtypeStruct((8, 2, 4, 2, 16, 128), BF16),
        in_specs=[hbm, hbm, hbm],
        out_specs=hbm,
        scratch_shapes=[
            pltpu.VMEM((2, 4, 4, 2, 128, 128), BF16),
            pltpu.VMEM((128, 512), BF16),
            pltpu.SMEM((2, 16), F32),
            pltpu.VMEM((4, 8, 4, 16, 128), BF16),
            pltpu.VMEM((4, 4, 4, 2, 16, 128), BF16),
            pltpu.VMEM((4, 4, 4, 2, 16, 128), BF16),
            pltpu.VMEM((2, 4, 256, 1024), BF16),
            pltpu.VMEM((4, 2, 4, 256, 128), BF16),
            pltpu.VMEM((4, 512, 512), BF16),
            pltpu.VMEM((256, 512), F32),
            pltpu.VMEM((32, 4, 16, 128), BF16),
            pltpu.VMEM((8, 2, 4, 2, 16, 128), BF16),
            dma((2, 4)),
            dma(()),
            dma(()),
            dma((4,)),
            dma((4,)),
            dma((2, 2)),
            dma(()),
            dma((13,)),
            dma((3, 2, 4)),
            dma((2, 2)),
            dma((2, 4)),
            dma((2,)),
            dma((2, 4)),
            dma((4,)),
            dma((2,)),
        ],
        compiler_params=pltpu.CompilerParams(
            collective_id=0, has_side_effects=True, vmem_limit_bytes=VMEM_LIMIT
        ),
        name="exchange",
    )(traces.reshape(4, 8, 2, 128, 128), jnp.asarray(forward), source_inverse)
    return pl.pallas_call(
        restore_kernel,
        out_shape=jax.ShapeDtypeStruct(traces.shape, BF16),
        in_specs=[hbm, hbm],
        out_specs=hbm,
        scratch_shapes=[
            pltpu.VMEM((2, 8, 2, 4, 16, 128), BF16),
            pltpu.VMEM((128, 512), BF16),
            pltpu.VMEM((4, width, 128), BF16),
            dma((2,)),
            dma(()),
            dma((8,)),
        ],
        compiler_params=pltpu.CompilerParams(vmem_limit_bytes=VMEM_LIMIT),
        name="restore",
    )(spectra, jnp.asarray(backward))


def solution(mesh):
    forward, backward = tables(16, 128)
    in_specs = (P(("freq", "row", "col"), None, None), P())
    out_specs = P(("freq", "row", "col"), None, None)
    return jax.shard_map(
        functools.partial(on_device, forward, backward),
        mesh=mesh,
        in_specs=in_specs,
        out_specs=out_specs,
        check_vma=False,
    )
```
